256 devices in a mesh: event: 16 (over x_hi, z), lon: 16 (over y, x_lo, core).
Axes of the slice: x: 4 (x_hi: 2, x_lo: 2; x = x_hi * 2 + x_lo), y: 4, z: 8, core: 2. Of those that a mesh axis runs over, the one named last changes fastest.
Arguments:
- adjoint_init: bfloat16 [16, 9, 16, 512, 128], P('event', None, None, 'lon'), may hold values from -6 to 6
- forward_state: bfloat16 [16, 8, 9, 16, 512, 128], P('event', None, None, None, 'lon'), may hold values from -3 to 3
- p_speed: float32 [16, 512, 128], P(None, 'lon'), may hold values from 0.3 to 0.5
- s_speed: float32 [16, 512, 128], P(None, 'lon'), may hold values from 0.1 to 0.2
- density: float32 [16, 512, 128], P(None, 'lon'), may hold values from 0.8 to 1.6
Outputs:
- kernels: float32 [3, 16, 512, 128], P(None, 'event', 'lon')
The draws below stay inside these ranges and needn't reach their ends.
All inputs are finite; a program needn't handle non-finite values.
Results may differ from the reference program's by a relative error of at most 0.015.
Values may be sent and summed in bfloat16 or wider, within the bound.
No kernel may reach another device: no remote copies, remote signals or barrier semaphores. Data moves between devices by JAX's collectives and lax.ppermute only.
A program may use at most 64 MiB of HBM per device.

```python
import jax
import jax.numpy as jnp
from jax import lax

LAT = 128
LEV = 16
STEPS = 8
EVENTS = 16
NLON = 512


def raised(values, own_key, source, target, shards_of, factor):
    owner, partner = [(jnp.arange(values.shape[position]) // (values.shape[position] // shards_of)).reshape([-1 if axis == position else 1 for axis in range(values.ndim)]) for position in (source, target)]
    chosen = jax.random.permutation(own_key, shards_of)[partner]
    strong = (owner == chosen) | (owner == (partner + shards_of // 2) % shards_of)
    return jnp.where(strong, factor * values, values)


def shard_levels(stream_key, dims, shards, low, high):
    def one(axis_at, shards_of):
        heights = jax.random.uniform(jax.random.fold_in(jax.random.fold_in(stream_key, 6), axis_at), (shards_of,), jnp.float32, low / len(shards), high / len(shards))
        return jnp.repeat(jnp.exp(heights), dims[axis_at] // shards_of).reshape((-1,) + (1,) * (len(dims) - axis_at - 1))

    loudness = one(*shards[0])
    for cut in shards[1:]:
        loudness = loudness * one(*cut)
    return loudness


def centred(own_key, shape, scale, reach, pieces=(), held_as=jnp.bfloat16):
    factor_of = shard_levels(own_key, shape, pieces, -0.22, 0.18) if pieces else 1.0
    result = jax.random.normal(own_key, shape, jnp.float32) * scale * factor_of
    return jnp.minimum(jnp.maximum(result, -reach), reach).astype(held_as)


def bell_draw_with(own_key, dims, deviation, most, pieces, heavy, dtype=jnp.bfloat16):
    result = deviation * jax.random.normal(own_key, dims, jnp.float32)
    if pieces:
        result = result * shard_levels(own_key, dims, pieces, -0.22, 0.18)
    return jnp.clip(raised(result, jax.random.fold_in(own_key, 3), *heavy), -most, most).astype(dtype)


def setup_inputs(seed: int = 0) -> dict:
    key_list = jax.random.split(jax.random.key(seed), 6)
    return {
        "adjoint_init": centred(key_list[0], (EVENTS, 9, LEV, NLON, LAT), 1.0, 6.0, ((0, 16), (3, 16))),
        "forward_state": bell_draw_with(key_list[1], (EVENTS, STEPS, 9, LEV, NLON, LAT), 0.5, 3.0, ((0, 16), (4, 16)), (0, 3, 16, 2.0)),
        "p_speed": jnp.clip(0.3 + 0.19999999 * jax.random.uniform(key_list[2], (LEV, NLON, LAT), jnp.float32) ** shard_levels(key_list[2], (LEV, NLON, LAT), ((1, 16),), -0.2, 0.2), 0.3, 0.5),
        "s_speed": jnp.clip(0.1 + 0.1 * jax.random.uniform(key_list[3], (LEV, NLON, LAT), jnp.float32) ** shard_levels(key_list[3], (LEV, NLON, LAT), ((1, 16),), -0.2, 0.2), 0.1, 0.2),
        "density": jnp.clip(0.8 + 0.8 * jax.random.uniform(key_list[4], (LEV, NLON, LAT), jnp.float32) ** shard_levels(key_list[4], (LEV, NLON, LAT), ((1, 16),), -0.2, 0.2), 0.8, 1.6),
    }


def ahead_diff(values, along):
    length = values.shape[along]
    border = jnp.zeros_like(lax.slice_in_dim(values, 0, 1, axis=along))
    return jnp.concatenate([lax.slice_in_dim(values, 1, length, axis=along), border], axis=along) - values


def behind_diff(values, along):
    length = values.shape[along]
    border = jnp.zeros_like(lax.slice_in_dim(values, 0, 1, axis=along))
    return values - jnp.concatenate([border, lax.slice_in_dim(values, 0, length - 1, axis=along)], axis=along)


def cycle_ahead(values, along):
    return jnp.roll(values, -1, axis=along) - values


def cycle_behind(values, along):
    return values - jnp.roll(values, 1, axis=along)


def forcing(stress, lon_ahead, lon_behind):
    stress_xx, stress_yy, stress_zz, stress_xy, stress_xz, stress_yz = [stress[index].astype(jnp.float32) for index in range(6)]
    force_x = lon_ahead(stress_xx, 1) + behind_diff(stress_xy, 2) + behind_diff(stress_xz, 0)
    force_y = lon_behind(stress_xy, 1) + ahead_diff(stress_yy, 2) + behind_diff(stress_yz, 0)
    force_z = lon_behind(stress_xz, 1) + behind_diff(stress_yz, 2) + ahead_diff(stress_zz, 0)
    return force_x, force_y, force_z


def strain_rates(velocity, lon_ahead, lon_behind):
    speed_x, speed_y, speed_z = [velocity[index].astype(jnp.float32) for index in range(3)]
    rate_xx = lon_behind(speed_x, 1)
    rate_yy = behind_diff(speed_y, 2)
    rate_zz = behind_diff(speed_z, 0)
    rate_xy = 0.5 * (ahead_diff(speed_x, 2) + lon_ahead(speed_y, 1))
    rate_xz = 0.5 * (ahead_diff(speed_x, 0) + lon_ahead(speed_z, 1))
    rate_yz = 0.5 * (ahead_diff(speed_y, 0) + ahead_diff(speed_z, 2))
    return rate_xx, rate_yy, rate_zz, rate_xy, rate_xz, rate_yz


def update_stress(stress, strain_rate, lame_coef, shear_coef):
    rate_xx, rate_yy, rate_zz, rate_xy, rate_xz, rate_yz = strain_rate
    trace_rate = rate_xx + rate_yy + rate_zz
    twice_shear = 2.0 * shear_coef
    volume_part = lame_coef * trace_rate
    updated = [
        stress[0].astype(jnp.float32) + volume_part + twice_shear * rate_xx,
        stress[1].astype(jnp.float32) + volume_part + twice_shear * rate_yy,
        stress[2].astype(jnp.float32) + volume_part + twice_shear * rate_zz,
        stress[3].astype(jnp.float32) + twice_shear * rate_xy,
        stress[4].astype(jnp.float32) + twice_shear * rate_xz,
        stress[5].astype(jnp.float32) + twice_shear * rate_yz,
    ]
    return jnp.stack([item.astype(jnp.bfloat16) for item in updated])


def kernel_terms(velocity, strain_rate, forward_now):
    rate_xx, rate_yy, rate_zz, rate_xy, rate_xz, rate_yz = strain_rate
    forward_f = [forward_now[index].astype(jnp.float32) for index in range(9)]
    trace_rate = rate_xx + rate_yy + rate_zz
    lame_term = trace_rate * (forward_f[3] + forward_f[4] + forward_f[5])
    shear_term = 2.0 * (rate_xx * forward_f[3] + rate_yy * forward_f[4] + rate_zz * forward_f[5]
                        + 2.0 * (rate_xy * forward_f[6] + rate_xz * forward_f[7] + rate_yz * forward_f[8]))
    speed = [velocity[index].astype(jnp.float32) for index in range(3)]
    density_term = speed[0] * forward_f[0] + speed[1] * forward_f[1] + speed[2] * forward_f[2]
    return lame_term, shear_term, density_term


def combine_kernels(kernel_total, p_speed, s_speed, density):
    lame_coef = density * (p_speed * p_speed - 2.0 * s_speed * s_speed)
    shear_coef = density * s_speed * s_speed
    return jnp.stack([
        2.0 * density * p_speed * p_speed * kernel_total[0],
        2.0 * density * s_speed * s_speed * (kernel_total[1] - 2.0 * kernel_total[0]),
        density * kernel_total[2] + lame_coef * kernel_total[0] + shear_coef * kernel_total[1],
    ])


def reference(adjoint_init, forward_state, p_speed, s_speed, density):
    lame_coef = density * (p_speed * p_speed - 2.0 * s_speed * s_speed)
    shear_coef = density * s_speed * s_speed
    buoyancy = 1.0 / density

    def advance(state_pair, forward_now):
        fields, kernel_sums = state_pair
        force = forcing(fields[3:9], cycle_ahead, cycle_behind)
        velocity = jnp.stack([(fields[index].astype(jnp.float32) + buoyancy * force[index]).astype(jnp.bfloat16) for index in range(3)])
        strain_rate = strain_rates(velocity, cycle_ahead, cycle_behind)
        stress = update_stress(fields[3:9], strain_rate, lame_coef, shear_coef)
        kernel_sums = kernel_sums + jnp.stack(kernel_terms(velocity, strain_rate, forward_now))
        return (jnp.concatenate([velocity, stress]), kernel_sums), None

    def per_event(event_total, event_inputs):
        initial, forward = event_inputs
        blank_sums = jnp.zeros((3,) + p_speed.shape, jnp.float32)
        (final_fields, kernel_sums), unused = lax.scan(advance, (initial, blank_sums), forward)
        return event_total + kernel_sums, None

    kernel_total, unused = lax.scan(per_event, jnp.zeros((3,) + p_speed.shape, jnp.float32), (adjoint_init, forward_state))
    return combine_kernels(kernel_total, p_speed, s_speed, density)
```

```python
import functools

import jax
import jax.numpy as jnp
from jax import lax
from jax.experimental import pallas as pl
from jax.experimental.pallas import tpu as pltpu
from jax.sharding import PartitionSpec as P

F32, BF16 = jnp.float32, jnp.bfloat16
HALO = 8
VX, VY, VZ, XX, YY, ZZ, XY, XZ, YZ = range(9)
LAME, SHEAR2, BUOY = range(3)


def propagate(steps, levels, width, init, left, right, coef, forward, out, state, mat, sums):
    wide = width + 2 * HALO
    step = pl.program_id(0)
    lane = lax.broadcasted_iota(jnp.int32, (8, 128), 1)
    row_chunks = [(HALO, 8, None)]
    row_chunks += [(2 * HALO + start, 16, start) for start in range(0, width, 16)]
    row_chunks += [(2 * HALO + width, 8, None)]

    @pl.when(step == 0)
    def _():
        zero_level = jnp.zeros((9, 1, wide + 16, 128), F32)
        state[:, pl.ds(0, 1)] = zero_level
        state[:, pl.ds(levels + 1, 1)] = zero_level

        def load(level, carry):
            for field in range(9):
                state[field, level + 1, pl.ds(0, 8)] = jnp.zeros((8, 128), F32)
                state[field, level + 1, pl.ds(wide + 8, 8)] = jnp.zeros((8, 128), F32)
                state[field, level + 1, pl.ds(8, HALO)] = left[field, level].astype(F32)
                state[field, level + 1, pl.ds(8 + HALO, width)] = init[field, level].astype(F32)
                state[field, level + 1, pl.ds(8 + HALO + width, HALO)] = right[field, level].astype(F32)
            for which in range(3):
                mat[which, level, pl.ds(0, HALO)] = left[9 + which, level].astype(F32)
                mat[which, level, pl.ds(HALO, width)] = coef[which, level]
                mat[which, level, pl.ds(HALO + width, HALO)] = right[9 + which, level].astype(F32)
                sums[which, level] = jnp.zeros((width, 128), F32)
            return carry

        lax.fori_loop(0, levels, load, 0)

    def before_lat(value):
        edge = lax.broadcasted_iota(jnp.int32, value.shape, 1) == 0
        return jnp.where(edge, 0.0, pltpu.roll(value, 1, 1))

    def after_lat(value):
        edge = lax.broadcasted_iota(jnp.int32, value.shape, 1) == 127
        return jnp.where(edge, 0.0, pltpu.roll(value, 127, 1))

    def rounded(value):
        return value.astype(BF16).astype(F32)

    def velocity(level):
        for start, rows, own in row_chunks:
            def at(field, lev=0, lon=0):
                return state[field, level + 1 + lev, pl.ds(start + lon, rows)]

            xx, yy, zz, xy, xz, yz = [at(field) for field in range(3, 9)]
            force_x = (at(XX, lon=1) - xx) + (xy - before_lat(xy)) + (xz - at(XZ, lev=-1))
            force_y = (xy - at(XY, lon=-1)) + (after_lat(yy) - yy) + (yz - at(YZ, lev=-1))
            force_z = (xz - at(XZ, lon=-1)) + (yz - before_lat(yz)) + (at(ZZ, lev=1) - zz)
            buoy = mat[BUOY, level, pl.ds(start - 8, rows)]
            for field, force in ((VX, force_x), (VY, force_y), (VZ, force_z)):
                state[field, level + 1, pl.ds(start, rows)] = rounded(at(field) + buoy * force)

    def stress(level):
        for start, rows, own in row_chunks:
            def at(field, lev=0, lon=0):
                return state[field, level + 1 + lev, pl.ds(start + lon, rows)]

            vx, vy, vz = at(VX), at(VY), at(VZ)
            e_xx = vx - at(VX, lon=-1)
            e_yy = vy - before_lat(vy)
            e_zz = vz - at(VZ, lev=-1)
            d_xy = (after_lat(vx) - vx) + (at(VY, lon=1) - vy)
            d_xz = (at(VX, lev=1) - vx) + (at(VZ, lon=1) - vz)
            d_yz = (at(VY, lev=1) - vy) + (after_lat(vz) - vz)
            trace = e_xx + e_yy + e_zz
            lame = mat[LAME, level, pl.ds(start - 8, rows)]
            shear2 = mat[SHEAR2, level, pl.ds(start - 8, rows)]
            shear = 0.5 * shear2
            volume = lame * trace
            for field, change in (
                (XX, volume + shear2 * e_xx),
                (YY, volume + shear2 * e_yy),
                (ZZ, volume + shear2 * e_zz),
                (XY, shear * d_xy),
                (XZ, shear * d_xz),
                (YZ, shear * d_yz),
            ):
                state[field, level + 1, pl.ds(start, rows)] = rounded(at(field) + change)
            if own is not None:
                f = [forward[0, 0, field, level, pl.ds(own, rows)].astype(F32) for field in range(9)]
                mine = pl.ds(own, rows)
                sums[0, level, mine] += trace * (f[3] + f[4] + f[5])
                sums[1, level, mine] += (e_xx * f[3] + e_yy * f[4] + e_zz * f[5]) + (
                    d_xy * f[6] + d_xz * f[7] + d_yz * f[8]
                )
                sums[2, level, mine] += vx * f[0] + vy * f[1] + vz * f[2]

    velocity(0)

    def sweep(level, carry):
        velocity(level + 1)
        stress(level)
        return carry

    lax.fori_loop(0, levels - 1, sweep, 0)
    stress(levels - 1)

    @pl.when(step == steps - 1)
    def _():
        def store(level, carry):
            out[level, 0] = sums[0, level].astype(BF16)
            out[level, 1] = (2.0 * sums[1, level]).astype(BF16)
            out[level, 2] = sums[2, level].astype(BF16)
            return carry

        lax.fori_loop(0, levels, store, 0)


def run_steps(init, left, right, coef, forward):
    _, steps, _, levels, width, lat = forward.shape
    wide = width + 2 * HALO
    whole = lambda array: pl.BlockSpec(array.shape, lambda t, n=array.ndim: (0,) * n)
    return pl.pallas_call(
        functools.partial(propagate, steps, levels, width),
        grid=(steps,),
        in_specs=[
            whole(init),
            whole(left),
            whole(right),
            whole(coef),
            pl.BlockSpec((1, 1, 9, levels, width, lat), lambda t: (0, t, 0, 0, 0, 0)),
        ],
        out_specs=pl.BlockSpec((levels, 3, width, lat), lambda t: (0, 0, 0, 0)),
        out_shape=jax.ShapeDtypeStruct((levels, 3, width, lat), BF16),
        scratch_shapes=[
            pltpu.VMEM((9, levels + 2, wide + 16, lat), F32),
            pltpu.VMEM((3, levels, wide, lat), F32),
            pltpu.VMEM((3, levels, width, lat), F32),
        ],
        compiler_params=pltpu.CompilerParams(vmem_limit_bytes=48 * 1024 * 1024),
    )(init, left, right, coef, forward)


def combine_kernels(total, p_speed, s_speed, density):
    lame = density * (p_speed * p_speed - 2.0 * s_speed * s_speed)
    shear = density * s_speed * s_speed
    return jnp.stack(
        [
            2.0 * density * p_speed * p_speed * total[0],
            2.0 * density * s_speed * s_speed * (total[1] - 2.0 * total[0]),
            density * total[2] + lame * total[0] + shear * total[1],
        ]
    )


def shards(adjoint_init, forward_state, p_speed, s_speed, density):
    init = adjoint_init[0]
    width = init.shape[2]
    lame = density * (p_speed * p_speed - 2.0 * s_speed * s_speed)
    shear2 = 2.0 * density * s_speed * s_speed
    coef = jnp.stack([lame, shear2, 1.0 / density])

    def edge(start):
        return jnp.concatenate(
            [init[:, :, start : start + HALO], coef[:, :, start : start + HALO].astype(BF16)]
        )

    count = lax.axis_size("lon")
    up = [(i, (i + 1) % count) for i in range(count)]
    left = lax.ppermute(edge(width - HALO), "lon", up)
    right = lax.ppermute(edge(0), "lon", [(j, i) for i, j in up])
    partial = run_steps(init, left, right, coef, forward_state)
    parts = lax.all_to_all(partial, "event", 0, 0, tiled=True)
    total = jnp.sum(parts.astype(F32), axis=0, keepdims=False)[:, None]
    first_row = lax.axis_index("event")
    own = [lax.dynamic_slice_in_dim(item, first_row, 1, 0) for item in (p_speed, s_speed, density)]
    return combine_kernels(total, *own)


def solution(mesh):
    placed = (
        P("event", None, None, "lon", None),
        P("event", None, None, None, "lon", None),
        P(None, "lon", None),
        P(None, "lon", None),
        P(None, "lon", None),
    )
    return jax.shard_map(
        shards, mesh=mesh, in_specs=placed, out_specs=P(None, "event", "lon", None), check_vma=False
    )
```

```python
import functools

import jax
import jax.numpy as jnp
from jax import lax
from jax.experimental import pallas as pl
from jax.experimental.pallas import tpu as pltpu
from jax.sharding import PartitionSpec as P

F32, BF16 = jnp.float32, jnp.bfloat16
HALO = 8
PAD = 8
VX, VY, VZ, XX, YY, ZZ, XY, XZ, YZ = range(9)
LAME, SHEAR2, BUOY = range(3)


def before_lat(value):
    edge = lax.broadcasted_iota(jnp.int32, value.shape, 1) == 0
    return jnp.where(edge, 0.0, pltpu.roll(value, 1, 1))


def after_lat(value):
    edge = lax.broadcasted_iota(jnp.int32, value.shape, 1) == 127
    return jnp.where(edge, 0.0, pltpu.roll(value, 127, 1))


def rounded(value):
    return value.astype(BF16).astype(F32)


def push(at, put, buoy):
    x_buoy, shift, yz_buoy = buoy
    xy, xz = at(XY, 0, shift), at(XZ, 0, shift)
    xy_x, xz_x = at(XY, 0, 0), at(XZ, 0, 0)
    yz = at(YZ, 0, shift)
    force_x = (at(XX, 0, 1) - at(XX, 0, 0)) + (xy_x - before_lat(xy_x)) + (xz_x - at(XZ, -1, 0))
    yy = at(YY, 0, shift)
    force_y = (xy - at(XY, 0, shift - 1)) + (after_lat(yy) - yy) + (yz - at(YZ, -1, shift))
    force_z = (
        (xz - at(XZ, 0, shift - 1))
        + (yz - before_lat(yz))
        + (at(ZZ, 1, shift) - at(ZZ, 0, shift))
    )
    put(VX, 0, rounded(at(VX, 0, 0) + x_buoy * force_x))
    put(VY, shift, rounded(at(VY, 0, shift) + yz_buoy * force_y))
    put(VZ, shift, rounded(at(VZ, 0, shift) + yz_buoy * force_z))


def strain(at, put, lame, shear2):
    vx, vy, vz = at(VX, 0, 0), at(VY, 0, 0), at(VZ, 0, 0)
    e_xx = vx - at(VX, 0, -1)
    e_yy = vy - before_lat(vy)
    e_zz = vz - at(VZ, -1, 0)
    d_xy = (after_lat(vx) - vx) + (at(VY, 0, 1) - vy)
    d_xz = (at(VX, 1, 0) - vx) + (at(VZ, 0, 1) - vz)
    d_yz = (at(VY, 1, 0) - vy) + (after_lat(vz) - vz)
    trace = e_xx + e_yy + e_zz
    shear = 0.5 * shear2
    volume = lame * trace
    for field, change in (
        (XX, volume + shear2 * e_xx),
        (YY, volume + shear2 * e_yy),
        (ZZ, volume + shear2 * e_zz),
        (XY, shear * d_xy),
        (XZ, shear * d_xz),
        (YZ, shear * d_yz),
    ):
        put(field, 0, rounded(at(field, 0, 0) + change))
    return (vx, vy, vz), (e_xx, e_yy, e_zz, d_xy, d_xz, d_yz), trace


def terms(speed, rate, trace, f):
    return (
        trace * (f[3] + f[4] + f[5]),
        (rate[0] * f[3] + rate[1] * f[4] + rate[2] * f[5])
        + (rate[3] * f[6] + rate[4] * f[7] + rate[5] * f[8]),
        speed[0] * f[0] + speed[1] * f[1] + speed[2] * f[2],
    )


def inner(steps, levels, width, init, coef, forward, sums, stair, state):
    step = pl.program_id(0)

    def keep(level, side, field, row, value):
        stair[side, field, level, pl.ds(row, 1)] = value

    @pl.when(step == 0)
    def _():
        empty = jnp.zeros((9, 1, width + 2 * PAD, 128), F32)
        state[:, pl.ds(0, 1)] = empty
        state[:, pl.ds(levels + 1, 1)] = empty

        def load(level, carry):
            for field in range(9):
                state[field, level + 1, pl.ds(0, PAD)] = jnp.zeros((PAD, 128), F32)
                state[field, level + 1, pl.ds(PAD + width, PAD)] = jnp.zeros((PAD, 128), F32)
                state[field, level + 1, pl.ds(PAD, width)] = init[field, level].astype(F32)
                stair[0, field, level] = jnp.zeros((16, 128), F32)
                stair[1, field, level] = jnp.zeros((16, 128), F32)
                if field != VX:
                    stair[0, field, level, pl.ds(0, 1)] = state[field, level + 1, pl.ds(PAD, 1)]
                if field not in (VY, VZ):
                    stair[1, field, level, pl.ds(15, 1)] = state[field, level + 1, pl.ds(PAD + width - 1, 1)]
            for which in range(3):
                sums[which, level] = jnp.zeros((width, 128), F32)
            return carry

        lax.fori_loop(0, levels, load, 0)

    def view(level, start, rows):
        def at(field, lev, lon):
            return state[field, level + 1 + lev, pl.ds(PAD + start + lon, rows)]

        def put(field, lon, value):
            state[field, level + 1, pl.ds(PAD + start + lon, rows)] = value

        return at, put

    def velocity(level):
        for start in range(0, width, 16):
            buoy = coef[BUOY, level, pl.ds(start, 16)]
            push(*view(level, start, 16), (buoy, 0, buoy))
        for field in (VX, VY, VZ):
            first = step if field == VX else step + 1
            last = 30 - step if field == VX else 31 - step
            keep(level, 0, field, first, state[field, level + 1, pl.ds(PAD + first, 1)])
            keep(level, 1, field, last - 16, state[field, level + 1, pl.ds(PAD + last, 1)])

    def stress(level):
        for start in range(0, width, 16):
            mine = pl.ds(start, 16)
            parts = strain(*view(level, start, 16), coef[LAME, level, mine], coef[SHEAR2, level, mine])
            f = [forward[0, 0, field, level, mine].astype(F32) for field in range(9)]
            column = start + lax.broadcasted_iota(jnp.int32, (16, 128), 0)
            right = (column > step) & (column < width - 1 - step)
            for which, term in enumerate(terms(*parts, f)):
                sums[which, level, mine] += jnp.where(right, term, 0.0)
        for field in range(3, 9):
            keep(level, 0, field, step + 1, state[field, level + 1, pl.ds(PAD + step + 1, 1)])
            keep(level, 1, field, 14 - step, state[field, level + 1, pl.ds(PAD + 30 - step, 1)])

    velocity(0)
    for level in range(levels):
        if level + 1 < levels:
            velocity(level + 1)
        stress(level)


def outer(steps, levels, width, left, right, coef, forward, first_sums, stair, out, state, mat, sums, wide_f):
    step = pl.program_id(0)

    @pl.when(step == 0)
    def _():
        for side in range(2):
            empty = jnp.zeros((9, 1, 24, 128), F32)
            state[side, :, pl.ds(0, 1)] = empty
            state[side, :, pl.ds(levels + 1, 1)] = empty

        def load(level, carry):
            for field in range(9):
                halo = left[field, level].astype(F32)
                state[0, field, level + 1, pl.ds(8, 16)] = stair[0, field, level]
                state[0, field, level + 1, pl.ds(0, 8)] = halo
                state[1, field, level + 1, pl.ds(0, 16)] = stair[1, field, level]
                state[1, field, level + 1, pl.ds(16, 8)] = right[field, level].astype(F32)
                wide_f[0, field, level, pl.ds(0, 8)] = jnp.zeros((8, 128), F32)
                wide_f[1, field, level, pl.ds(8, 8)] = jnp.zeros((8, 128), F32)
            for which in range(3):
                mat[0, which, level, pl.ds(0, 8)] = left[9 + which, level].astype(F32)
                mat[0, which, level, pl.ds(8, 16)] = coef[which, level, pl.ds(0, 16)]
                mat[1, which, level, pl.ds(0, 16)] = coef[which, level, pl.ds(width - 16, 16)]
                mat[1, which, level, pl.ds(16, 8)] = right[9 + which, level].astype(F32)
                sums[which, level, pl.ds(0, 8)] = jnp.zeros((8, 128), F32)
                sums[which, level, pl.ds(8, width)] = first_sums[which, level]
                sums[which, level, pl.ds(8 + width, 8)] = jnp.zeros((8, 128), F32)
            return carry

        lax.fori_loop(0, levels, load, 0)

    places = ((step, step + 1, step + 1), (15 - step, 15 - step, 39 - step))

    def view(side, level, start):
        def at(field, lev, lon):
            return state[side, field, level + 1 + lev, pl.ds(start + lon, 8)]

        def put(field, lon, value):
            state[side, field, level + 1, pl.ds(start + lon, 8)] = value

        return at, put

    def velocity(level):
        for side in range(2):
            start = places[side][0]
            x_buoy = mat[side, BUOY, level, pl.ds(start, 8)]
            yz_buoy = mat[side, BUOY, level, pl.ds(start + 1, 8)]
            push(*view(side, level, start), (x_buoy, 1, yz_buoy))

    def stress(level):
        for side in range(2):
            _, start, place = places[side]
            rows = pl.ds(start, 8)
            parts = strain(*view(side, level, start), mat[side, LAME, level, rows], mat[side, SHEAR2, level, rows])
            own = pl.ds(0, 16) if side == 0 else pl.ds(width - 16, 16)
            for field in range(9):
                value = forward[0, 0, field, level, own].astype(F32)
                if side == 0:
                    wide_f[side, field, level, pl.ds(8, 8)] = value[:8]
                else:
                    wide_f[side, field, level, pl.ds(0, 8)] = value[8:]
            where_f = step + 1 if side == 0 else 7 - step
            f = [wide_f[side, field, level, pl.ds(where_f, 8)] for field in range(9)]
            for which, term in enumerate(terms(*parts, f)):
                sums[which, level, pl.ds(place, 8)] += term

    velocity(0)
    for level in range(levels):
        if level + 1 < levels:
            velocity(level + 1)
        stress(level)

    @pl.when(step == steps - 1)
    def _():
        def store(level, carry):
            for which, factor in enumerate((1.0, 2.0, 1.0)):
                out[level, which] = (factor * sums[which, level, pl.ds(8, width)]).astype(BF16)
            return carry

        lax.fori_loop(0, levels, store, 0)


def whole(array):
    return pl.BlockSpec(array.shape, lambda t, n=len(array.shape): (0,) * n)


def run_inner(init, coef, forward):
    _, steps, _, levels, width, lat = forward.shape
    outs = [
        jax.ShapeDtypeStruct((3, levels, width, lat), F32),
        jax.ShapeDtypeStruct((2, 9, levels, 16, lat), F32),
    ]
    return pl.pallas_call(
        functools.partial(inner, steps, levels, width),
        grid=(steps,),
        in_specs=[
            whole(init),
            whole(coef),
            pl.BlockSpec((1, 1, 9, levels, width, lat), lambda t: (0, t, 0, 0, 0, 0)),
        ],
        out_specs=[whole(item) for item in outs],
        out_shape=outs,
        scratch_shapes=[pltpu.VMEM((9, levels + 2, width + 2 * PAD, lat), F32)],
        compiler_params=pltpu.CompilerParams(vmem_limit_bytes=30 * 1024 * 1024),
        cost_estimate=pl.CostEstimate(flops=60_000_000, bytes_accessed=30_000_000, transcendentals=0),
    )(init, coef, forward)


def run_outer(left, right, coef, forward, first_sums, stair):
    _, steps, _, levels, width, lat = forward.shape
    out = jax.ShapeDtypeStruct((levels, 3, width, lat), BF16)
    return pl.pallas_call(
        functools.partial(outer, steps, levels, width),
        grid=(steps,),
        in_specs=[
            whole(left),
            whole(right),
            whole(coef),
            pl.BlockSpec((1, 1, 9, levels, width, lat), lambda t: (0, t, 0, 0, 0, 0)),
            whole(first_sums),
            whole(stair),
        ],
        out_specs=whole(out),
        out_shape=out,
        scratch_shapes=[
            pltpu.VMEM((2, 9, levels + 2, 24, lat), F32),
            pltpu.VMEM((2, 3, levels, 24, lat), F32),
            pltpu.VMEM((3, levels, width + 16, lat), F32),
            pltpu.VMEM((2, 9, levels, 16, lat), F32),
        ],
        compiler_params=pltpu.CompilerParams(vmem_limit_bytes=40 * 1024 * 1024),
        cost_estimate=pl.CostEstimate(flops=30_000_000, bytes_accessed=20_000_000, transcendentals=0),
    )(left, right, coef, forward, first_sums, stair)


def combine_kernels(total, p_speed, s_speed, density):
    lame = density * (p_speed * p_speed - 2.0 * s_speed * s_speed)
    shear = density * s_speed * s_speed
    return jnp.stack(
        [
            2.0 * density * p_speed * p_speed * total[0],
            2.0 * density * s_speed * s_speed * (total[1] - 2.0 * total[0]),
            density * total[2] + lame * total[0] + shear * total[1],
        ]
    )


def shards(adjoint_init, forward_state, p_speed, s_speed, density):
    init = adjoint_init[0]
    width = init.shape[2]
    lame = density * (p_speed * p_speed - 2.0 * s_speed * s_speed)
    shear2 = 2.0 * density * s_speed * s_speed
    coef = jnp.stack([lame, shear2, 1.0 / density])

    def edge(start):
        return jnp.concatenate(
            [init[:, :, start : start + HALO], coef[:, :, start : start + HALO].astype(BF16)]
        )

    count = lax.axis_size("lon")
    up = [(i, (i + 1) % count) for i in range(count)]
    left = lax.ppermute(edge(width - HALO), "lon", up)
    right = lax.ppermute(edge(0), "lon", [(j, i) for i, j in up])
    first_sums, stair = run_inner(init, coef, forward_state)
    partial = run_outer(left, right, coef, forward_state, first_sums, stair)
    parts = lax.all_to_all(partial, "event", 0, 0, tiled=True)
    total = jnp.sum(parts.astype(F32), axis=0, keepdims=False)[:, None]
    first_row = lax.axis_index("event")
    own = [lax.dynamic_slice_in_dim(item, first_row, 1, 0) for item in (p_speed, s_speed, density)]
    return combine_kernels(total, *own)


def solution(mesh):
    placed = (
        P("event", None, None, "lon", None),
        P("event", None, None, None, "lon", None),
        P(None, "lon", None),
        P(None, "lon", None),
        P(None, "lon", None),
    )
    return jax.shard_map(
        shards, mesh=mesh, in_specs=placed, out_specs=P(None, "event", "lon", None), check_vma=False
    )
```

```python
import functools

import jax
import jax.numpy as jnp
from jax import lax
from jax.experimental import pallas as pl
from jax.experimental.pallas import tpu as pltpu
from jax.sharding import PartitionSpec as P

F32, BF16 = jnp.float32, jnp.bfloat16
HALO = 8
PAD = 8
FRONT = 8
VX, VY, VZ, XX, YY, ZZ, XY, XZ, YZ = range(9)
LAME, SHEAR2, BUOY = range(3)


def before_lat(value):
    edge = lax.broadcasted_iota(jnp.int32, value.shape, 1) == 0
    return jnp.where(edge, 0.0, pltpu.roll(value, 1, 1))


def after_lat(value):
    edge = lax.broadcasted_iota(jnp.int32, value.shape, 1) == 127
    return jnp.where(edge, 0.0, pltpu.roll(value, 127, 1))


def rounded(value):
    return value.astype(BF16).astype(F32)


def push(at, put, buoy):
    x_buoy, shift, yz_buoy = buoy
    xy, xz = at(XY, 0, shift), at(XZ, 0, shift)
    xy_x, xz_x = at(XY, 0, 0), at(XZ, 0, 0)
    yz = at(YZ, 0, shift)
    force_x = (at(XX, 0, 1) - at(XX, 0, 0)) + (xy_x - before_lat(xy_x)) + (xz_x - at(XZ, -1, 0))
    yy = at(YY, 0, shift)
    force_y = (xy - at(XY, 0, shift - 1)) + (after_lat(yy) - yy) + (yz - at(YZ, -1, shift))
    force_z = (
        (xz - at(XZ, 0, shift - 1))
        + (yz - before_lat(yz))
        + (at(ZZ, 1, shift) - at(ZZ, 0, shift))
    )
    put(VX, 0, rounded(at(VX, 0, 0) + x_buoy * force_x))
    put(VY, shift, rounded(at(VY, 0, shift) + yz_buoy * force_y))
    put(VZ, shift, rounded(at(VZ, 0, shift) + yz_buoy * force_z))


def strain(at, put, lame, shear2):
    vx, vy, vz = at(VX, 0, 0), at(VY, 0, 0), at(VZ, 0, 0)
    e_xx = vx - at(VX, 0, -1)
    e_yy = vy - before_lat(vy)
    e_zz = vz - at(VZ, -1, 0)
    d_xy = (after_lat(vx) - vx) + (at(VY, 0, 1) - vy)
    d_xz = (at(VX, 1, 0) - vx) + (at(VZ, 0, 1) - vz)
    d_yz = (at(VY, 1, 0) - vy) + (after_lat(vz) - vz)
    trace = e_xx + e_yy + e_zz
    shear = 0.5 * shear2
    volume = lame * trace
    for field, change in (
        (XX, volume + shear2 * e_xx),
        (YY, volume + shear2 * e_yy),
        (ZZ, volume + shear2 * e_zz),
        (XY, shear * d_xy),
        (XZ, shear * d_xz),
        (YZ, shear * d_yz),
    ):
        put(field, 0, rounded(at(field, 0, 0) + change))
    return (vx, vy, vz), (e_xx, e_yy, e_zz, d_xy, d_xz, d_yz), trace


def terms(speed, rate, trace, f):
    return (
        trace * (f[3] + f[4] + f[5]),
        (rate[0] * f[3] + rate[1] * f[4] + rate[2] * f[5])
        + (rate[3] * f[6] + rate[4] * f[7] + rate[5] * f[8]),
        speed[0] * f[0] + speed[1] * f[1] + speed[2] * f[2],
    )


def inner(steps, levels, width, init, coef, forward, sums, stair, state):
    step = pl.program_id(0)

    def keep(level, side, field, row, value):
        stair[side, field, level, pl.ds(row, 1)] = value

    @pl.when(step == 0)
    def _():
        empty = jnp.zeros((9, 1, width + 2 * PAD, 128), F32)
        state[:, pl.ds(0, 1)] = empty
        state[:, pl.ds(levels + 1, 1)] = empty

        def load(level, carry):
            for field in range(9):
                state[field, level + 1, pl.ds(0, PAD)] = jnp.zeros((PAD, 128), F32)
                state[field, level + 1, pl.ds(PAD + width, PAD)] = jnp.zeros((PAD, 128), F32)
                state[field, level + 1, pl.ds(PAD, width)] = init[field, level].astype(F32)
                stair[0, field, level] = jnp.zeros((16, 128), F32)
                stair[1, field, level] = jnp.zeros((16, 128), F32)
                if field != VX:
                    stair[0, field, level, pl.ds(0, 1)] = state[field, level + 1, pl.ds(PAD, 1)]
                if field not in (VY, VZ):
                    stair[1, field, level, pl.ds(15, 1)] = state[field, level + 1, pl.ds(PAD + width - 1, 1)]
            for which in range(3):
                sums[which, level] = jnp.zeros((width, 128), F32)
            return carry

        lax.fori_loop(0, levels, load, 0)

    def view(level, start, rows):
        def at(field, lev, lon):
            return state[field, level + 1 + lev, pl.ds(PAD + start + lon, rows)]

        def put(field, lon, value):
            state[field, level + 1, pl.ds(PAD + start + lon, rows)] = value

        return at, put

    def velocity(level):
        for start in range(0, width, 16):
            buoy = coef[BUOY, level, pl.ds(start, 16)]
            push(*view(level, start, 16), (buoy, 0, buoy))
        for field in (VX, VY, VZ):
            first = step if field == VX else step + 1
            last = 30 - step if field == VX else 31 - step
            keep(level, 0, field, first, state[field, level + 1, pl.ds(PAD + first, 1)])
            keep(level, 1, field, last - 16, state[field, level + 1, pl.ds(PAD + last, 1)])

    def stress(level):
        for start in range(0, width, 16):
            mine = pl.ds(start, 16)
            parts = strain(*view(level, start, 16), coef[LAME, level, mine], coef[SHEAR2, level, mine])
            f = [forward[0, 0, field, level, mine].astype(F32) for field in range(9)]
            column = start + lax.broadcasted_iota(jnp.int32, (16, 128), 0)
            right = (column > step) & (column < width - 1 - step)
            for which, term in enumerate(terms(*parts, f)):
                sums[which, level, mine] += jnp.where(right, term, 0.0)
        for field in range(3, 9):
            keep(level, 0, field, step + 1, state[field, level + 1, pl.ds(PAD + step + 1, 1)])
            keep(level, 1, field, 14 - step, state[field, level + 1, pl.ds(PAD + 30 - step, 1)])

    velocity(0)
    for level in range(levels):
        if level + 1 < levels:
            velocity(level + 1)
        stress(level)


def outer(steps, levels, width, left, right, coef, forward, first_sums, stair, out, state, mat, sums, wide_f):
    step = pl.program_id(0)

    @pl.when(step == 0)
    def _():
        for side in range(2):
            empty = jnp.zeros((9, 1, 24, 128), F32)
            state[side, :, pl.ds(0, 1)] = empty
            state[side, :, pl.ds(levels + 1, 1)] = empty

        def load(level, carry):
            for field in range(9):
                state[0, field, level + 1, pl.ds(FRONT, 8)] = left[field, level].astype(F32)
                state[0, field, level + 1, pl.ds(FRONT + 8, 8)] = stair[0, field, level, pl.ds(0, 8)]
                state[1, field, level + 1, pl.ds(0, 8)] = stair[1, field, level, pl.ds(8, 8)]
                state[1, field, level + 1, pl.ds(FRONT, 8)] = right[field, level].astype(F32)
                wide_f[0, field, level, pl.ds(0, 8)] = jnp.zeros((8, 128), F32)
                wide_f[1, field, level, pl.ds(8, 8)] = jnp.zeros((8, 128), F32)
            for which in range(3):
                mat[0, which, level, pl.ds(0, 8)] = left[9 + which, level].astype(F32)
                mat[0, which, level, pl.ds(8, 16)] = coef[which, level, pl.ds(0, 16)]
                mat[1, which, level, pl.ds(0, 16)] = coef[which, level, pl.ds(width - 16, 16)]
                mat[1, which, level, pl.ds(16, 8)] = right[9 + which, level].astype(F32)
                for side in range(2):
                    sums[side, which, level] = jnp.zeros((24, 128), F32)
            return carry

        lax.fori_loop(0, levels, load, 0)

    def widen(level):
        for field in range(9):
            wide_f[0, field, level, pl.ds(8, 8)] = forward[0, 0, field, level, pl.ds(0, 16)].astype(F32)[:8]
            wide_f[1, field, level, pl.ds(0, 8)] = forward[0, 0, field, level, pl.ds(width - 16, 16)].astype(F32)[8:]

    for level in range(levels):
        widen(level)

    old_x, new_x, old_s = (0, -1), (-1, 0), (1, -1)
    x_coef, s_coef, f_row = (step, 15 - step), (step + 1, 15 - step), (step + 1, 7 - step)

    def velocity(level):
        for side in range(2):

            def at(field, lev, lon):
                return state[side, field, level + 1 + lev, pl.ds(FRONT + old_x[side] + lon, 8)]

            def put(field, lon, value):
                state[side, field, level + 1, pl.ds(FRONT + new_x[side] + lon, 8)] = value

            x_buoy = mat[side, BUOY, level, pl.ds(x_coef[side], 8)]
            yz_buoy = mat[side, BUOY, level, pl.ds(x_coef[side] + 1, 8)]
            push(at, put, (x_buoy, 1, yz_buoy))
        for field in (VX, VY, VZ):
            first, row = (step, 7) if field == VX else (step + 1, 8)
            state[0, field, level + 1, pl.ds(FRONT + row, 1)] = stair[0, field, level, pl.ds(first, 1)]
            last, row = (14 - step, -1) if field == VX else (15 - step, 0)
            state[1, field, level + 1, pl.ds(FRONT + row, 1)] = stair[1, field, level, pl.ds(last, 1)]

    def stress(level):
        for side in range(2):

            def at(field, lev, lon):
                row = FRONT + lon + (old_s[side] if field >= 3 else 0)
                return state[side, field, level + 1 + lev, pl.ds(row, 8)]

            def put(field, lon, value):
                state[side, field, level + 1, pl.ds(FRONT + lon, 8)] = value

            rows = pl.ds(s_coef[side], 8)
            parts = strain(at, put, mat[side, LAME, level, rows], mat[side, SHEAR2, level, rows])
            f = [wide_f[side, field, level, pl.ds(f_row[side], 8)] for field in range(9)]
            for which, term in enumerate(terms(*parts, f)):
                before = sums[side, which, level, pl.ds(8 + old_s[side], 8)]
                sums[side, which, level, pl.ds(8, 8)] = before + term
        for field in range(3, 9):
            state[0, field, level + 1, pl.ds(FRONT + 8, 1)] = stair[0, field, level, pl.ds(step + 1, 1)]
            state[1, field, level + 1, pl.ds(FRONT - 1, 1)] = stair[1, field, level, pl.ds(14 - step, 1)]

    velocity(0)
    for level in range(levels):
        if level + 1 < levels:
            velocity(level + 1)
        stress(level)

    @pl.when(step == steps - 1)
    def _():
        def store(level, carry):
            for which, factor in enumerate((1.0, 2.0, 1.0)):
                total = first_sums[which, level]
                ends = [sums[side, which, level, pl.ds(8, 8)] for side in range(2)]
                total = jnp.concatenate([total[:8] + ends[0], total[8:-8], total[-8:] + ends[1]])
                out[level, which] = (factor * total).astype(BF16)
            return carry

        lax.fori_loop(0, levels, store, 0)


def whole(array):
    return pl.BlockSpec(array.shape, lambda t, n=len(array.shape): (0,) * n)


def run_inner(init, coef, forward):
    _, steps, _, levels, width, lat = forward.shape
    outs = [
        jax.ShapeDtypeStruct((3, levels, width, lat), F32),
        jax.ShapeDtypeStruct((2, 9, levels, 16, lat), F32),
    ]
    return pl.pallas_call(
        functools.partial(inner, steps, levels, width),
        grid=(steps,),
        in_specs=[
            whole(init),
            whole(coef),
            pl.BlockSpec((1, 1, 9, levels, width, lat), lambda t: (0, t, 0, 0, 0, 0)),
        ],
        out_specs=[whole(item) for item in outs],
        out_shape=outs,
        scratch_shapes=[pltpu.VMEM((9, levels + 2, width + 2 * PAD, lat), F32)],
        compiler_params=pltpu.CompilerParams(vmem_limit_bytes=30 * 1024 * 1024),
        cost_estimate=pl.CostEstimate(flops=60_000_000, bytes_accessed=30_000_000, transcendentals=0),
    )(init, coef, forward)


def run_outer(left, right, coef, forward, first_sums, stair):
    _, steps, _, levels, width, lat = forward.shape
    out = jax.ShapeDtypeStruct((levels, 3, width, lat), BF16)
    return pl.pallas_call(
        functools.partial(outer, steps, levels, width),
        grid=(steps,),
        in_specs=[
            whole(left),
            whole(right),
            whole(coef),
            pl.BlockSpec((1, 1, 9, levels, width, lat), lambda t: (0, t, 0, 0, 0, 0)),
            whole(first_sums),
            whole(stair),
        ],
        out_specs=whole(out),
        out_shape=out,
        scratch_shapes=[
            pltpu.VMEM((2, 9, levels + 2, 24, lat), F32),
            pltpu.VMEM((2, 3, levels, 24, lat), F32),
            pltpu.VMEM((2, 3, levels, 24, lat), F32),
            pltpu.VMEM((2, 9, levels, 16, lat), F32),
        ],
        compiler_params=pltpu.CompilerParams(vmem_limit_bytes=40 * 1024 * 1024),
        cost_estimate=pl.CostEstimate(flops=30_000_000, bytes_accessed=20_000_000, transcendentals=0),
    )(left, right, coef, forward, first_sums, stair)


def combine_kernels(total, p_speed, s_speed, density):
    lame = density * (p_speed * p_speed - 2.0 * s_speed * s_speed)
    shear = density * s_speed * s_speed
    return jnp.stack(
        [
            2.0 * density * p_speed * p_speed * total[0],
            2.0 * density * s_speed * s_speed * (total[1] - 2.0 * total[0]),
            density * total[2] + lame * total[0] + shear * total[1],
        ]
    )


def shards(adjoint_init, forward_state, p_speed, s_speed, density):
    init = adjoint_init[0]
    width = init.shape[2]
    lame = density * (p_speed * p_speed - 2.0 * s_speed * s_speed)
    shear2 = 2.0 * density * s_speed * s_speed
    coef = jnp.stack([lame, shear2, 1.0 / density])

    def edge(start):
        return jnp.concatenate(
            [init[:, :, start : start + HALO], coef[:, :, start : start + HALO].astype(BF16)]
        )

    count = lax.axis_size("lon")
    up = [(i, (i + 1) % count) for i in range(count)]
    left = lax.ppermute(edge(width - HALO), "lon", up)
    right = lax.ppermute(edge(0), "lon", [(j, i) for i, j in up])
    first_sums, stair = run_inner(init, coef, forward_state)
    partial = run_outer(left, right, coef, forward_state, first_sums, stair)
    parts = lax.all_to_all(partial, "event", 0, 0, tiled=True)
    total = jnp.sum(parts.astype(F32), axis=0, keepdims=False)[:, None]
    first_row = lax.axis_index("event")
    own = [lax.dynamic_slice_in_dim(item, first_row, 1, 0) for item in (p_speed, s_speed, density)]
    return combine_kernels(total, *own)


def solution(mesh):
    placed = (
        P("event", None, None, "lon", None),
        P("event", None, None, None, "lon", None),
        P(None, "lon", None),
        P(None, "lon", None),
        P(None, "lon", None),
    )
    return jax.shard_map(
        shards, mesh=mesh, in_specs=placed, out_specs=P(None, "event", "lon", None), check_vma=False
    )
```

```python
import functools

import jax
import jax.numpy as jnp
from jax import lax
from jax.experimental import pallas as pl
from jax.experimental.pallas import tpu as pltpu
from jax.sharding import PartitionSpec as P

F32, BF16 = jnp.float32, jnp.bfloat16
HALO = 8
PAD = 8
FRONT = 8
VX, VY, VZ, XX, YY, ZZ, XY, XZ, YZ = range(9)
LAME, SHEAR2, BUOY = range(3)


def before_lat(value):
    edge = lax.broadcasted_iota(jnp.int32, value.shape, 1) == 0
    return jnp.where(edge, 0.0, pltpu.roll(value, 1, 1))


def after_lat(value):
    edge = lax.broadcasted_iota(jnp.int32, value.shape, 1) == 127
    return jnp.where(edge, 0.0, pltpu.roll(value, 127, 1))


def rounded(value):
    return value.astype(BF16).astype(F32)


def push(at, put, buoy):
    x_buoy, shift, yz_buoy = buoy
    xy, xz = at(XY, 0, shift), at(XZ, 0, shift)
    xy_x, xz_x = at(XY, 0, 0), at(XZ, 0, 0)
    yz = at(YZ, 0, shift)
    force_x = (at(XX, 0, 1) - at(XX, 0, 0)) + (xy_x - before_lat(xy_x)) + (xz_x - at(XZ, -1, 0))
    yy = at(YY, 0, shift)
    force_y = (xy - at(XY, 0, shift - 1)) + (after_lat(yy) - yy) + (yz - at(YZ, -1, shift))
    force_z = (
        (xz - at(XZ, 0, shift - 1))
        + (yz - before_lat(yz))
        + (at(ZZ, 1, shift) - at(ZZ, 0, shift))
    )
    put(VX, 0, rounded(at(VX, 0, 0) + x_buoy * force_x))
    put(VY, shift, rounded(at(VY, 0, shift) + yz_buoy * force_y))
    put(VZ, shift, rounded(at(VZ, 0, shift) + yz_buoy * force_z))


def strain(at, put, lame, shear2):
    vx, vy, vz = at(VX, 0, 0), at(VY, 0, 0), at(VZ, 0, 0)
    e_xx = vx - at(VX, 0, -1)
    e_yy = vy - before_lat(vy)
    e_zz = vz - at(VZ, -1, 0)
    d_xy = (after_lat(vx) - vx) + (at(VY, 0, 1) - vy)
    d_xz = (at(VX, 1, 0) - vx) + (at(VZ, 0, 1) - vz)
    d_yz = (at(VY, 1, 0) - vy) + (after_lat(vz) - vz)
    trace = e_xx + e_yy + e_zz
    shear = 0.5 * shear2
    volume = lame * trace
    for field, change in (
        (XX, volume + shear2 * e_xx),
        (YY, volume + shear2 * e_yy),
        (ZZ, volume + shear2 * e_zz),
        (XY, shear * d_xy),
        (XZ, shear * d_xz),
        (YZ, shear * d_yz),
    ):
        put(field, 0, rounded(at(field, 0, 0) + change))
    return (vx, vy, vz), (e_xx, e_yy, e_zz, d_xy, d_xz, d_yz), trace


def terms(speed, rate, trace, f):
    return (
        trace * (f[3] + f[4] + f[5]),
        (rate[0] * f[3] + rate[1] * f[4] + rate[2] * f[5])
        + (rate[3] * f[6] + rate[4] * f[7] + rate[5] * f[8]),
        speed[0] * f[0] + speed[1] * f[1] + speed[2] * f[2],
    )


def inner(steps, levels, width, init, coef, forward, sums, stair, state):
    step = pl.program_id(0)

    def keep(level, side, field, row, value):
        stair[side, field, level, pl.ds(row, 1)] = value

    @pl.when(step == 0)
    def _():
        empty = jnp.zeros((9, 1, width + 2 * PAD, 128), F32)
        state[:, pl.ds(0, 1)] = empty
        state[:, pl.ds(levels + 1, 1)] = empty

        def load(level, carry):
            for field in range(9):
                state[field, level + 1, pl.ds(0, PAD)] = jnp.zeros((PAD, 128), F32)
                state[field, level + 1, pl.ds(PAD + width, PAD)] = jnp.zeros((PAD, 128), F32)
                state[field, level + 1, pl.ds(PAD, width)] = init[field, level].astype(F32)
                stair[0, field, level] = jnp.zeros((16, 128), F32)
                stair[1, field, level] = jnp.zeros((16, 128), F32)
                if field != VX:
                    stair[0, field, level, pl.ds(0, 1)] = state[field, level + 1, pl.ds(PAD, 1)]
                if field not in (VY, VZ):
                    stair[1, field, level, pl.ds(15, 1)] = state[field, level + 1, pl.ds(PAD + width - 1, 1)]
            for which in range(3):
                sums[which, level] = jnp.zeros((width, 128), F32)
            return carry

        lax.fori_loop(0, levels, load, 0)

    def view(level, start, rows):
        def at(field, lev, lon):
            return state[field, level + 1 + lev, pl.ds(PAD + start + lon, rows)]

        def put(field, lon, value):
            state[field, level + 1, pl.ds(PAD + start + lon, rows)] = value

        return at, put

    def velocity(level):
        for start in range(0, width, 16):
            buoy = coef[BUOY, level, pl.ds(start, 16)]
            push(*view(level, start, 16), (buoy, 0, buoy))
        for field in (VX, VY, VZ):
            first = step if field == VX else step + 1
            last = 30 - step if field == VX else 31 - step
            keep(level, 0, field, first, state[field, level + 1, pl.ds(PAD + first, 1)])
            keep(level, 1, field, last - 16, state[field, level + 1, pl.ds(PAD + last, 1)])

    def stress(level):
        for start in range(0, width, 16):
            mine = pl.ds(start, 16)
            parts = strain(*view(level, start, 16), coef[LAME, level, mine], coef[SHEAR2, level, mine])
            f = [forward[0, 0, field, level, mine].astype(F32) for field in range(9)]
            column = start + lax.broadcasted_iota(jnp.int32, (16, 128), 0)
            right = (column > step) & (column < width - 1 - step)
            for which, term in enumerate(terms(*parts, f)):
                sums[which, level, mine] += jnp.where(right, term, 0.0)
        for field in range(3, 9):
            keep(level, 0, field, step + 1, state[field, level + 1, pl.ds(PAD + step + 1, 1)])
            keep(level, 1, field, 14 - step, state[field, level + 1, pl.ds(PAD + 30 - step, 1)])

    velocity(0)
    for level in range(levels):
        if level + 1 < levels:
            velocity(level + 1)
        stress(level)


def outer(steps, levels, width, left, right, coef, forward, first_sums, stair, out, state, mat, sums, wide_f):
    step = pl.program_id(0)

    @pl.when(step == 0)
    def _():
        for side in range(2):
            empty = jnp.zeros((9, 1, 24, 128), F32)
            state[side, :, pl.ds(0, 1)] = empty
            state[side, :, pl.ds(levels + 1, 1)] = empty

        def load(level, carry):
            for field in range(9):
                state[0, field, level + 1, pl.ds(FRONT, 8)] = left[field, level].astype(F32)
                state[0, field, level + 1, pl.ds(FRONT + 8, 8)] = stair[0, field, level, pl.ds(0, 8)]
                state[1, field, level + 1, pl.ds(0, 8)] = stair[1, field, level, pl.ds(8, 8)]
                state[1, field, level + 1, pl.ds(FRONT, 8)] = right[field, level].astype(F32)
                wide_f[0, field, level, pl.ds(0, 8)] = jnp.zeros((8, 128), F32)
                wide_f[1, field, level, pl.ds(8, 8)] = jnp.zeros((8, 128), F32)
            for which in range(3):
                mat[0, which, level, pl.ds(0, 8)] = left[9 + which, level].astype(F32)
                mat[0, which, level, pl.ds(8, 16)] = coef[which, level, pl.ds(0, 16)]
                mat[1, which, level, pl.ds(0, 16)] = coef[which, level, pl.ds(width - 16, 16)]
                mat[1, which, level, pl.ds(16, 8)] = right[9 + which, level].astype(F32)
                for side in range(2):
                    sums[side, which, level] = jnp.zeros((24, 128), F32)
            return carry

        lax.fori_loop(0, levels, load, 0)

    def widen(level):
        for field in range(9):
            wide_f[0, field, level, pl.ds(8, 8)] = forward[0, 0, field, level, pl.ds(0, 16)].astype(F32)[:8]
            wide_f[1, field, level, pl.ds(0, 8)] = forward[0, 0, field, level, pl.ds(width - 16, 16)].astype(F32)[8:]

    for level in range(levels):
        widen(level)

    old_x, new_x, old_s = (0, -1), (-1, 0), (1, -1)
    x_coef, s_coef, f_row = (step, 15 - step), (step + 1, 15 - step), (step + 1, 7 - step)

    def velocity(level):
        for side in range(2):

            def at(field, lev, lon):
                return state[side, field, level + 1 + lev, pl.ds(FRONT + old_x[side] + lon, 8)]

            def put(field, lon, value):
                state[side, field, level + 1, pl.ds(FRONT + new_x[side] + lon, 8)] = value

            x_buoy = mat[side, BUOY, level, pl.ds(x_coef[side], 8)]
            yz_buoy = mat[side, BUOY, level, pl.ds(x_coef[side] + 1, 8)]
            push(at, put, (x_buoy, 1, yz_buoy))
        for field in (VX, VY, VZ):
            first, row = (step, 7) if field == VX else (step + 1, 8)
            state[0, field, level + 1, pl.ds(FRONT + row, 1)] = stair[0, field, level, pl.ds(first, 1)]
            last, row = (14 - step, -1) if field == VX else (15 - step, 0)
            state[1, field, level + 1, pl.ds(FRONT + row, 1)] = stair[1, field, level, pl.ds(last, 1)]

    def stress(level):
        for side in range(2):

            def at(field, lev, lon):
                row = FRONT + lon + (old_s[side] if field >= 3 else 0)
                return state[side, field, level + 1 + lev, pl.ds(row, 8)]

            def put(field, lon, value):
                state[side, field, level + 1, pl.ds(FRONT + lon, 8)] = value

            rows = pl.ds(s_coef[side], 8)
            parts = strain(at, put, mat[side, LAME, level, rows], mat[side, SHEAR2, level, rows])
            f = [wide_f[side, field, level, pl.ds(f_row[side], 8)] for field in range(9)]
            for which, term in enumerate(terms(*parts, f)):
                before = sums[side, which, level, pl.ds(8 + old_s[side], 8)]
                sums[side, which, level, pl.ds(8, 8)] = before + term
        for field in range(3, 9):
            state[0, field, level + 1, pl.ds(FRONT + 8, 1)] = stair[0, field, level, pl.ds(step + 1, 1)]
            state[1, field, level + 1, pl.ds(FRONT - 1, 1)] = stair[1, field, level, pl.ds(14 - step, 1)]

    velocity(0)
    for level in range(levels):
        if level + 1 < levels:
            velocity(level + 1)
        stress(level)

    @pl.when(step == steps - 1)
    def _():
        def store(level, carry):
            for which, factor in enumerate((1.0, 2.0, 1.0)):
                total = first_sums[which, level]
                ends = [sums[side, which, level, pl.ds(8, 8)] for side in range(2)]
                total = jnp.concatenate([total[:8] + ends[0], total[8:-8], total[-8:] + ends[1]])
                out[level, which] = (factor * total).astype(BF16)
            return carry

        lax.fori_loop(0, levels, store, 0)


def prepare(levels, width, row, init, p_speed, s_speed, density, first, last, coef, own):
    def load(level, carry):
        rho, p, s = density[level], p_speed[level], s_speed[level]
        parts = (rho * (p * p - 2.0 * s * s), 2.0 * rho * s * s, 1.0 / rho)
        for which, part in enumerate(parts):
            coef[which, level] = part
            first[9 + which, level] = part[:HALO].astype(BF16)
            last[9 + which, level] = part[width - HALO :].astype(BF16)
        for field in range(9):
            first[field, level] = init[field, level, pl.ds(0, 16)].astype(F32)[:HALO].astype(BF16)
            last[field, level] = init[field, level, pl.ds(width - 16, 16)].astype(F32)[16 - HALO :].astype(BF16)
        return carry

    lax.fori_loop(0, levels, load, 0, unroll=4)
    for which, item in enumerate((p_speed, s_speed, density)):
        own[which] = item[row[0]]


def finish(events, parts, own, out):
    total = [parts[0, which].astype(F32) for which in range(3)]
    for event in range(1, events):
        total = [so_far + parts[event, which].astype(F32) for which, so_far in enumerate(total)]
    p_speed, s_speed, density = own[0], own[1], own[2]
    lame = density * (p_speed * p_speed - 2.0 * s_speed * s_speed)
    shear = density * s_speed * s_speed
    out[0, 0] = 2.0 * density * p_speed * p_speed * total[0]
    out[1, 0] = 2.0 * density * s_speed * s_speed * (total[1] - 2.0 * total[0])
    out[2, 0] = density * total[2] + lame * total[0] + shear * total[1]


IN_VMEM = pl.BlockSpec(memory_space=pltpu.VMEM)
MEBI = 1024 * 1024


def run_prepare(row, init, p_speed, s_speed, density):
    _, levels, width, lat = init.shape
    edge = jax.ShapeDtypeStruct((12, levels, HALO, lat), BF16)
    return pl.pallas_call(
        functools.partial(prepare, levels, width),
        in_specs=[pl.BlockSpec(memory_space=pltpu.SMEM)] + [IN_VMEM] * 4,
        out_specs=[IN_VMEM] * 4,
        out_shape=[
            edge,
            edge,
            jax.ShapeDtypeStruct((3, levels, width, lat), F32),
            jax.ShapeDtypeStruct((3, width, lat), F32),
        ],
        compiler_params=pltpu.CompilerParams(vmem_limit_bytes=16 * MEBI),
    )(row, init, p_speed, s_speed, density)


def run_finish(parts, own):
    events, _, width, lat = parts.shape
    return pl.pallas_call(
        functools.partial(finish, events),
        in_specs=[IN_VMEM] * 2,
        out_specs=IN_VMEM,
        out_shape=jax.ShapeDtypeStruct((3, 1, width, lat), F32),
        compiler_params=pltpu.CompilerParams(vmem_limit_bytes=8 * MEBI),
    )(parts, own)


def by_step(forward):
    return pl.BlockSpec((1, 1) + forward.shape[2:], lambda t: (0, t, 0, 0, 0, 0))


def run_inner(init, coef, forward):
    _, steps, _, levels, width, lat = forward.shape
    outs = [
        jax.ShapeDtypeStruct((3, levels, width, lat), F32),
        jax.ShapeDtypeStruct((2, 9, levels, 16, lat), F32),
    ]
    return pl.pallas_call(
        functools.partial(inner, steps, levels, width),
        grid=(steps,),
        in_specs=[IN_VMEM, IN_VMEM, by_step(forward)],
        out_specs=[IN_VMEM] * 2,
        out_shape=outs,
        scratch_shapes=[pltpu.VMEM((9, levels + 2, width + 2 * PAD, lat), F32)],
        compiler_params=pltpu.CompilerParams(vmem_limit_bytes=46 * MEBI),
        cost_estimate=pl.CostEstimate(flops=60_000_000, bytes_accessed=30_000_000, transcendentals=0),
    )(init, coef, forward)


def run_outer(left, right, coef, forward, first_sums, stair):
    _, steps, _, levels, width, lat = forward.shape
    return pl.pallas_call(
        functools.partial(outer, steps, levels, width),
        grid=(steps,),
        in_specs=[IN_VMEM] * 3 + [by_step(forward)] + [IN_VMEM] * 2,
        out_specs=IN_VMEM,
        out_shape=jax.ShapeDtypeStruct((levels, 3, width, lat), BF16),
        scratch_shapes=[
            pltpu.VMEM((2, 9, levels + 2, 24, lat), F32),
            pltpu.VMEM((2, 3, levels, 24, lat), F32),
            pltpu.VMEM((2, 3, levels, 24, lat), F32),
            pltpu.VMEM((2, 9, levels, 16, lat), F32),
        ],
        compiler_params=pltpu.CompilerParams(vmem_limit_bytes=46 * MEBI),
        cost_estimate=pl.CostEstimate(flops=30_000_000, bytes_accessed=20_000_000, transcendentals=0),
    )(left, right, coef, forward, first_sums, stair)


def shards(adjoint_init, forward_state, p_speed, s_speed, density):
    init = adjoint_init[0]
    row = lax.axis_index("event").reshape(1)
    first, last, coef, own = run_prepare(row, init, p_speed, s_speed, density)
    count = lax.axis_size("lon")
    up = [(i, (i + 1) % count) for i in range(count)]
    left = lax.ppermute(last, "lon", up)
    right = lax.ppermute(first, "lon", [(j, i) for i, j in up])
    first_sums, stair = run_inner(init, coef, forward_state)
    partial = run_outer(left, right, coef, forward_state, first_sums, stair)
    parts = lax.all_to_all(partial, "event", 0, 0, tiled=True)
    return run_finish(parts, own)


def solution(mesh):
    placed = (
        P("event", None, None, "lon", None),
        P("event", None, None, None, "lon", None),
        P(None, "lon", None),
        P(None, "lon", None),
        P(None, "lon", None),
    )
    return jax.shard_map(
        shards, mesh=mesh, in_specs=placed, out_specs=P(None, "event", "lon", None), check_vma=False
    )
```

```python
import functools

import jax
import jax.numpy as jnp
from jax import lax
from jax.experimental import pallas as pl
from jax.experimental.pallas import tpu as pltpu
from jax.sharding import PartitionSpec as P

F32, BF16 = jnp.float32, jnp.bfloat16
HALO = 8
PAD = 8
FRONT = 8
VX, VY, VZ, XX, YY, ZZ, XY, XZ, YZ = range(9)
LAME, SHEAR2, BUOY = range(3)


def before_lat(value):
    edge = lax.broadcasted_iota(jnp.int32, value.shape, 1) == 0
    return jnp.where(edge, 0.0, pltpu.roll(value, 1, 1))


def after_lat(value):
    edge = lax.broadcasted_iota(jnp.int32, value.shape, 1) == 127
    return jnp.where(edge, 0.0, pltpu.roll(value, 127, 1))


def rounded(value):
    return value.astype(BF16).astype(F32)


def push(at, put, buoy):
    x_buoy, shift, yz_buoy = buoy
    xy, xz = at(XY, 0, shift), at(XZ, 0, shift)
    xy_x, xz_x = at(XY, 0, 0), at(XZ, 0, 0)
    yz = at(YZ, 0, shift)
    force_x = (at(XX, 0, 1) - at(XX, 0, 0)) + (xy_x - before_lat(xy_x)) + (xz_x - at(XZ, -1, 0))
    yy = at(YY, 0, shift)
    force_y = (xy - at(XY, 0, shift - 1)) + (after_lat(yy) - yy) + (yz - at(YZ, -1, shift))
    force_z = (
        (xz - at(XZ, 0, shift - 1))
        + (yz - before_lat(yz))
        + (at(ZZ, 1, shift) - at(ZZ, 0, shift))
    )
    put(VX, 0, rounded(at(VX, 0, 0) + x_buoy * force_x))
    put(VY, shift, rounded(at(VY, 0, shift) + yz_buoy * force_y))
    put(VZ, shift, rounded(at(VZ, 0, shift) + yz_buoy * force_z))


def strain(at, put, lame, shear2):
    vx, vy, vz = at(VX, 0, 0), at(VY, 0, 0), at(VZ, 0, 0)
    e_xx = vx - at(VX, 0, -1)
    e_yy = vy - before_lat(vy)
    e_zz = vz - at(VZ, -1, 0)
    d_xy = (after_lat(vx) - vx) + (at(VY, 0, 1) - vy)
    d_xz = (at(VX, 1, 0) - vx) + (at(VZ, 0, 1) - vz)
    d_yz = (at(VY, 1, 0) - vy) + (after_lat(vz) - vz)
    trace = e_xx + e_yy + e_zz
    shear = 0.5 * shear2
    volume = lame * trace
    for field, change in (
        (XX, volume + shear2 * e_xx),
        (YY, volume + shear2 * e_yy),
        (ZZ, volume + shear2 * e_zz),
        (XY, shear * d_xy),
        (XZ, shear * d_xz),
        (YZ, shear * d_yz),
    ):
        put(field, 0, rounded(at(field, 0, 0) + change))
    return (vx, vy, vz), (e_xx, e_yy, e_zz, d_xy, d_xz, d_yz), trace


def terms(speed, rate, trace, f):
    return (
        trace * (f[3] + f[4] + f[5]),
        (rate[0] * f[3] + rate[1] * f[4] + rate[2] * f[5])
        + (rate[3] * f[6] + rate[4] * f[7] + rate[5] * f[8]),
        speed[0] * f[0] + speed[1] * f[1] + speed[2] * f[2],
    )


def inner(steps, levels, width, init, coef, forward_hbm, sums, stair, forward, state, arrived):
    step = pl.program_id(0)

    def fetch(which):
        return pltpu.make_async_copy(forward_hbm.at[0, which], forward.at[which], arrived.at[which])

    def keep(level, side, field, row, value):
        stair[side, field, level, pl.ds(row, 1)] = value

    @pl.when(step == 0)
    def _():
        for which in range(steps):
            fetch(which).start()
        empty = jnp.zeros((9, 1, width + 2 * PAD, 128), F32)
        state[:, pl.ds(0, 1)] = empty
        state[:, pl.ds(levels + 1, 1)] = empty

        def load(level, carry):
            for field in range(9):
                state[field, level + 1, pl.ds(0, PAD)] = jnp.zeros((PAD, 128), F32)
                state[field, level + 1, pl.ds(PAD + width, PAD)] = jnp.zeros((PAD, 128), F32)
                state[field, level + 1, pl.ds(PAD, width)] = init[field, level].astype(F32)
                stair[0, field, level] = jnp.zeros((16, 128), F32)
                stair[1, field, level] = jnp.zeros((16, 128), F32)
                if field != VX:
                    stair[0, field, level, pl.ds(0, 1)] = state[field, level + 1, pl.ds(PAD, 1)]
                if field not in (VY, VZ):
                    stair[1, field, level, pl.ds(15, 1)] = state[field, level + 1, pl.ds(PAD + width - 1, 1)]
            for which in range(3):
                sums[which, level] = jnp.zeros((width, 128), F32)
            return carry

        lax.fori_loop(0, levels, load, 0)

    def view(level, start, rows):
        def at(field, lev, lon):
            return state[field, level + 1 + lev, pl.ds(PAD + start + lon, rows)]

        def put(field, lon, value):
            state[field, level + 1, pl.ds(PAD + start + lon, rows)] = value

        return at, put

    def velocity(level):
        for start in range(0, width, 16):
            buoy = coef[BUOY, level, pl.ds(start, 16)]
            push(*view(level, start, 16), (buoy, 0, buoy))
        for field in (VX, VY, VZ):
            first = step if field == VX else step + 1
            last = 30 - step if field == VX else 31 - step
            keep(level, 0, field, first, state[field, level + 1, pl.ds(PAD + first, 1)])
            keep(level, 1, field, last - 16, state[field, level + 1, pl.ds(PAD + last, 1)])

    def stress(level):
        for start in range(0, width, 16):
            mine = pl.ds(start, 16)
            parts = strain(*view(level, start, 16), coef[LAME, level, mine], coef[SHEAR2, level, mine])
            f = [forward[step, field, level, mine].astype(F32) for field in range(9)]
            column = start + lax.broadcasted_iota(jnp.int32, (16, 128), 0)
            right = (column > step) & (column < width - 1 - step)
            for which, term in enumerate(terms(*parts, f)):
                sums[which, level, mine] += jnp.where(right, term, 0.0)
        for field in range(3, 9):
            keep(level, 0, field, step + 1, state[field, level + 1, pl.ds(PAD + step + 1, 1)])
            keep(level, 1, field, 14 - step, state[field, level + 1, pl.ds(PAD + 30 - step, 1)])

    fetch(step).wait()
    velocity(0)
    for level in range(levels):
        if level + 1 < levels:
            velocity(level + 1)
        stress(level)


def outer(steps, levels, width, left, right, coef, forward, first_sums, stair, out, state, mat, sums, wide_f):
    step = pl.program_id(0)

    @pl.when(step == 0)
    def _():
        for side in range(2):
            empty = jnp.zeros((9, 1, 24, 128), F32)
            state[side, :, pl.ds(0, 1)] = empty
            state[side, :, pl.ds(levels + 1, 1)] = empty

        def load(level, carry):
            for field in range(9):
                state[0, field, level + 1, pl.ds(FRONT, 8)] = left[field, level].astype(F32)
                state[0, field, level + 1, pl.ds(FRONT + 8, 8)] = stair[0, field, level, pl.ds(0, 8)]
                state[1, field, level + 1, pl.ds(0, 8)] = stair[1, field, level, pl.ds(8, 8)]
                state[1, field, level + 1, pl.ds(FRONT, 8)] = right[field, level].astype(F32)
                wide_f[0, field, level, pl.ds(0, 8)] = jnp.zeros((8, 128), F32)
                wide_f[1, field, level, pl.ds(8, 8)] = jnp.zeros((8, 128), F32)
            for which in range(3):
                mat[0, which, level, pl.ds(0, 8)] = left[9 + which, level].astype(F32)
                mat[0, which, level, pl.ds(8, 16)] = coef[which, level, pl.ds(0, 16)]
                mat[1, which, level, pl.ds(0, 16)] = coef[which, level, pl.ds(width - 16, 16)]
                mat[1, which, level, pl.ds(16, 8)] = right[9 + which, level].astype(F32)
                for side in range(2):
                    sums[side, which, level] = jnp.zeros((24, 128), F32)
            return carry

        lax.fori_loop(0, levels, load, 0)

    def widen(level):
        for field in range(9):
            wide_f[0, field, level, pl.ds(8, 8)] = forward[step, field, level, pl.ds(0, 16)].astype(F32)[:8]
            wide_f[1, field, level, pl.ds(0, 8)] = forward[step, field, level, pl.ds(width - 16, 16)].astype(F32)[8:]

    for level in range(levels):
        widen(level)

    old_x, new_x, old_s = (0, -1), (-1, 0), (1, -1)
    x_coef, s_coef, f_row = (step, 15 - step), (step + 1, 15 - step), (step + 1, 7 - step)

    def velocity(level):
        for side in range(2):

            def at(field, lev, lon):
                return state[side, field, level + 1 + lev, pl.ds(FRONT + old_x[side] + lon, 8)]

            def put(field, lon, value):
                state[side, field, level + 1, pl.ds(FRONT + new_x[side] + lon, 8)] = value

            x_buoy = mat[side, BUOY, level, pl.ds(x_coef[side], 8)]
            yz_buoy = mat[side, BUOY, level, pl.ds(x_coef[side] + 1, 8)]
            push(at, put, (x_buoy, 1, yz_buoy))
        for field in (VX, VY, VZ):
            first, row = (step, 7) if field == VX else (step + 1, 8)
            state[0, field, level + 1, pl.ds(FRONT + row, 1)] = stair[0, field, level, pl.ds(first, 1)]
            last, row = (14 - step, -1) if field == VX else (15 - step, 0)
            state[1, field, level + 1, pl.ds(FRONT + row, 1)] = stair[1, field, level, pl.ds(last, 1)]

    def stress(level):
        for side in range(2):

            def at(field, lev, lon):
                row = FRONT + lon + (old_s[side] if field >= 3 else 0)
                return state[side, field, level + 1 + lev, pl.ds(row, 8)]

            def put(field, lon, value):
                state[side, field, level + 1, pl.ds(FRONT + lon, 8)] = value

            rows = pl.ds(s_coef[side], 8)
            parts = strain(at, put, mat[side, LAME, level, rows], mat[side, SHEAR2, level, rows])
            f = [wide_f[side, field, level, pl.ds(f_row[side], 8)] for field in range(9)]
            for which, term in enumerate(terms(*parts, f)):
                before = sums[side, which, level, pl.ds(8 + old_s[side], 8)]
                sums[side, which, level, pl.ds(8, 8)] = before + term
        for field in range(3, 9):
            state[0, field, level + 1, pl.ds(FRONT + 8, 1)] = stair[0, field, level, pl.ds(step + 1, 1)]
            state[1, field, level + 1, pl.ds(FRONT - 1, 1)] = stair[1, field, level, pl.ds(14 - step, 1)]

    velocity(0)
    for level in range(levels):
        if level + 1 < levels:
            velocity(level + 1)
        stress(level)

    @pl.when(step == steps - 1)
    def _():
        def store(level, carry):
            for which, factor in enumerate((1.0, 2.0, 1.0)):
                total = first_sums[which, level]
                ends = [sums[side, which, level, pl.ds(8, 8)] for side in range(2)]
                total = jnp.concatenate([total[:8] + ends[0], total[8:-8], total[-8:] + ends[1]])
                out[level, which] = (factor * total).astype(BF16)
            return carry

        lax.fori_loop(0, levels, store, 0)


def prepare(levels, width, row, init, material, first, last, coef, own):
    def load(level, carry):
        p, s, rho = [material[which, level] for which in range(3)]
        parts = (rho * (p * p - 2.0 * s * s), 2.0 * rho * s * s, 1.0 / rho)
        for which, part in enumerate(parts):
            coef[which, level] = part
            first[9 + which, level] = part[:HALO].astype(BF16)
            last[9 + which, level] = part[width - HALO :].astype(BF16)
        for field in range(9):
            first[field, level] = init[field, level, pl.ds(0, 16)].astype(F32)[:HALO].astype(BF16)
            last[field, level] = init[field, level, pl.ds(width - 16, 16)].astype(F32)[16 - HALO :].astype(BF16)
        return carry

    lax.fori_loop(0, levels, load, 0, unroll=4)
    for which in range(3):
        own[which] = material[which, row[0]]


def finish(events, parts, own, out):
    total = [parts[0, which].astype(F32) for which in range(3)]
    for event in range(1, events):
        total = [so_far + parts[event, which].astype(F32) for which, so_far in enumerate(total)]
    p_speed, s_speed, density = own[0], own[1], own[2]
    lame = density * (p_speed * p_speed - 2.0 * s_speed * s_speed)
    shear = density * s_speed * s_speed
    out[0, 0] = 2.0 * density * p_speed * p_speed * total[0]
    out[1, 0] = 2.0 * density * s_speed * s_speed * (total[1] - 2.0 * total[0])
    out[2, 0] = density * total[2] + lame * total[0] + shear * total[1]


IN_VMEM = pl.BlockSpec(memory_space=pltpu.VMEM)
IN_HBM = pl.BlockSpec(memory_space=pltpu.HBM)
MEBI = 1024 * 1024


def run_prepare(row, init, material):
    _, levels, width, lat = init.shape
    edge = jax.ShapeDtypeStruct((12, levels, HALO, lat), BF16)
    return pl.pallas_call(
        functools.partial(prepare, levels, width),
        in_specs=[pl.BlockSpec(memory_space=pltpu.SMEM)] + [IN_VMEM] * 2,
        out_specs=[IN_VMEM] * 4,
        out_shape=[
            edge,
            edge,
            jax.ShapeDtypeStruct((3, levels, width, lat), F32),
            jax.ShapeDtypeStruct((3, width, lat), F32),
        ],
        compiler_params=pltpu.CompilerParams(vmem_limit_bytes=16 * MEBI),
    )(row, init, material)


def run_finish(parts, own):
    events, _, width, lat = parts.shape
    return pl.pallas_call(
        functools.partial(finish, events),
        in_specs=[IN_VMEM] * 2,
        out_specs=IN_VMEM,
        out_shape=jax.ShapeDtypeStruct((3, 1, width, lat), F32),
        compiler_params=pltpu.CompilerParams(vmem_limit_bytes=8 * MEBI),
    )(parts, own)


def run_inner(init, coef, forward):
    _, steps, _, levels, width, lat = forward.shape
    outs = [
        jax.ShapeDtypeStruct((3, levels, width, lat), F32),
        jax.ShapeDtypeStruct((2, 9, levels, 16, lat), F32),
        jax.ShapeDtypeStruct(forward.shape[1:], BF16),
    ]
    return pl.pallas_call(
        functools.partial(inner, steps, levels, width),
        grid=(steps,),
        in_specs=[IN_VMEM, IN_VMEM, IN_HBM],
        out_specs=[IN_VMEM] * 3,
        out_shape=outs,
        scratch_shapes=[
            pltpu.VMEM((9, levels + 2, width + 2 * PAD, lat), F32),
            pltpu.SemaphoreType.DMA((steps,)),
        ],
        compiler_params=pltpu.CompilerParams(vmem_limit_bytes=34 * MEBI),
        cost_estimate=pl.CostEstimate(flops=60_000_000, bytes_accessed=30_000_000, transcendentals=0),
    )(init, coef, forward)


def run_outer(left, right, coef, forward, first_sums, stair):
    steps, _, levels, width, lat = forward.shape
    return pl.pallas_call(
        functools.partial(outer, steps, levels, width),
        grid=(steps,),
        in_specs=[IN_VMEM] * 6,
        out_specs=IN_VMEM,
        out_shape=jax.ShapeDtypeStruct((levels, 3, width, lat), BF16),
        scratch_shapes=[
            pltpu.VMEM((2, 9, levels + 2, 24, lat), F32),
            pltpu.VMEM((2, 3, levels, 24, lat), F32),
            pltpu.VMEM((2, 3, levels, 24, lat), F32),
            pltpu.VMEM((2, 9, levels, 16, lat), F32),
        ],
        compiler_params=pltpu.CompilerParams(vmem_limit_bytes=34 * MEBI),
        cost_estimate=pl.CostEstimate(flops=30_000_000, bytes_accessed=20_000_000, transcendentals=0),
    )(left, right, coef, forward, first_sums, stair)


def shards(adjoint_init, forward_state, p_speed, s_speed, density):
    init = adjoint_init[0]
    row = lax.axis_index("event").reshape(1)
    first, last, coef, own = run_prepare(row, init, jnp.stack([p_speed, s_speed, density]))
    count = lax.axis_size("lon")
    up = [(i, (i + 1) % count) for i in range(count)]
    left = lax.ppermute(last, "lon", up)
    right = lax.ppermute(first, "lon", [(j, i) for i, j in up])
    first_sums, stair, forward = run_inner(init, coef, forward_state)
    partial = run_outer(left, right, coef, forward, first_sums, stair)
    parts = lax.all_to_all(partial, "event", 0, 0, tiled=True)
    return run_finish(parts, own)


def solution(mesh):
    placed = (
        P("event", None, None, "lon", None),
        P("event", None, None, None, "lon", None),
        P(None, "lon", None),
        P(None, "lon", None),
        P(None, "lon", None),
    )
    return jax.shard_map(
        shards, mesh=mesh, in_specs=placed, out_specs=P(None, "event", "lon", None), check_vma=False
    )
```

```python
import functools

import jax
import jax.numpy as jnp
from jax import lax
from jax.experimental import pallas as pl
from jax.experimental.pallas import tpu as pltpu
from jax.sharding import PartitionSpec as P

F32, BF16 = jnp.float32, jnp.bfloat16
HALO = 8
PAD = 8
FRONT = 8
VX, VY, VZ, XX, YY, ZZ, XY, XZ, YZ = range(9)
LAME, SHEAR2, BUOY = range(3)


def before_lat(value):
    edge = lax.broadcasted_iota(jnp.int32, value.shape, 1) == 0
    return jnp.where(edge, 0.0, pltpu.roll(value, 1, 1))


def after_lat(value):
    edge = lax.broadcasted_iota(jnp.int32, value.shape, 1) == 127
    return jnp.where(edge, 0.0, pltpu.roll(value, 127, 1))


def rounded(value):
    return value.astype(BF16).astype(F32)


def push(at, put, buoy):
    x_buoy, shift, yz_buoy = buoy
    xy, xz = at(XY, 0, shift), at(XZ, 0, shift)
    xy_x, xz_x = at(XY, 0, 0), at(XZ, 0, 0)
    yz = at(YZ, 0, shift)
    force_x = (at(XX, 0, 1) - at(XX, 0, 0)) + (xy_x - before_lat(xy_x)) + (xz_x - at(XZ, -1, 0))
    yy = at(YY, 0, shift)
    force_y = (xy - at(XY, 0, shift - 1)) + (after_lat(yy) - yy) + (yz - at(YZ, -1, shift))
    force_z = (
        (xz - at(XZ, 0, shift - 1))
        + (yz - before_lat(yz))
        + (at(ZZ, 1, shift) - at(ZZ, 0, shift))
    )
    put(VX, 0, rounded(at(VX, 0, 0) + x_buoy * force_x))
    put(VY, shift, rounded(at(VY, 0, shift) + yz_buoy * force_y))
    put(VZ, shift, rounded(at(VZ, 0, shift) + yz_buoy * force_z))


def strain(at, put, lame, shear2):
    vx, vy, vz = at(VX, 0, 0), at(VY, 0, 0), at(VZ, 0, 0)
    e_xx = vx - at(VX, 0, -1)
    e_yy = vy - before_lat(vy)
    e_zz = vz - at(VZ, -1, 0)
    d_xy = (after_lat(vx) - vx) + (at(VY, 0, 1) - vy)
    d_xz = (at(VX, 1, 0) - vx) + (at(VZ, 0, 1) - vz)
    d_yz = (at(VY, 1, 0) - vy) + (after_lat(vz) - vz)
    trace = e_xx + e_yy + e_zz
    shear = 0.5 * shear2
    volume = lame * trace
    for field, change in (
        (XX, volume + shear2 * e_xx),
        (YY, volume + shear2 * e_yy),
        (ZZ, volume + shear2 * e_zz),
        (XY, shear * d_xy),
        (XZ, shear * d_xz),
        (YZ, shear * d_yz),
    ):
        put(field, 0, rounded(at(field, 0, 0) + change))
    return (vx, vy, vz), (e_xx, e_yy, e_zz, d_xy, d_xz, d_yz), trace


def terms(speed, rate, trace, f):
    return (
        trace * (f[3] + f[4] + f[5]),
        (rate[0] * f[3] + rate[1] * f[4] + rate[2] * f[5])
        + (rate[3] * f[6] + rate[4] * f[7] + rate[5] * f[8]),
        speed[0] * f[0] + speed[1] * f[1] + speed[2] * f[2],
    )


def inner(steps, levels, width, half, init, coef, forward_hbm, sums, sent, kept, stair, forward, state, arrived):
    step = pl.program_id(0)

    def fetch(which):
        return pltpu.make_async_copy(forward_hbm.at[0, which], forward.at[which], arrived.at[which])

    def keep(level, side, field, row, value):
        stair[side, field, level, pl.ds(row, 1)] = value

    @pl.when(step == 0)
    def _():
        for which in range(steps):
            fetch(which).start()
        empty = jnp.zeros((9, 1, width + 2 * PAD, 128), F32)
        state[:, pl.ds(0, 1)] = empty
        state[:, pl.ds(levels + 1, 1)] = empty

        def load(level, carry):
            for field in range(9):
                state[field, level + 1, pl.ds(0, PAD)] = jnp.zeros((PAD, 128), F32)
                state[field, level + 1, pl.ds(PAD + width, PAD)] = jnp.zeros((PAD, 128), F32)
                state[field, level + 1, pl.ds(PAD, width)] = init[field, level].astype(F32)
                stair[0, field, level] = jnp.zeros((16, 128), F32)
                stair[1, field, level] = jnp.zeros((16, 128), F32)
                if field != VX:
                    stair[0, field, level, pl.ds(0, 1)] = state[field, level + 1, pl.ds(PAD, 1)]
                if field not in (VY, VZ):
                    stair[1, field, level, pl.ds(15, 1)] = state[field, level + 1, pl.ds(PAD + width - 1, 1)]
            for which in range(3):
                sums[which, level] = jnp.zeros((width, 128), F32)
            return carry

        lax.fori_loop(0, levels, load, 0)

    def view(level, start, rows):
        def at(field, lev, lon):
            return state[field, level + 1 + lev, pl.ds(PAD + start + lon, rows)]

        def put(field, lon, value):
            state[field, level + 1, pl.ds(PAD + start + lon, rows)] = value

        return at, put

    def velocity(level):
        for start in range(0, width, 16):
            buoy = coef[BUOY, level, pl.ds(start, 16)]
            push(*view(level, start, 16), (buoy, 0, buoy))
        for field in (VX, VY, VZ):
            first = step if field == VX else step + 1
            last = 30 - step if field == VX else 31 - step
            keep(level, 0, field, first, state[field, level + 1, pl.ds(PAD + first, 1)])
            keep(level, 1, field, last - 16, state[field, level + 1, pl.ds(PAD + last, 1)])

    def stress(level):
        for start in range(0, width, 16):
            mine = pl.ds(start, 16)
            parts = strain(*view(level, start, 16), coef[LAME, level, mine], coef[SHEAR2, level, mine])
            f = [forward[step, field, level, mine].astype(F32) for field in range(9)]
            column = start + lax.broadcasted_iota(jnp.int32, (16, 128), 0)
            right = (column > step) & (column < width - 1 - step)
            for which, term in enumerate(terms(*parts, f)):
                sums[which, level, mine] += jnp.where(right, term, 0.0)
        for field in range(3, 9):
            keep(level, 0, field, step + 1, state[field, level + 1, pl.ds(PAD + step + 1, 1)])
            keep(level, 1, field, 14 - step, state[field, level + 1, pl.ds(PAD + 30 - step, 1)])

    fetch(step).wait()
    velocity(0)
    for level in range(levels):
        if level + 1 < levels:
            velocity(level + 1)
        stress(level)

    @pl.when(step == steps - 1)
    def _():
        mine = pl.multiple_of(8 + 8 * half[0], 8)
        other = pl.multiple_of(16 - 8 * half[0], 8)
        for level in range(levels):
            for which in range(3):
                kept[which, level] = sums[which, level, pl.ds(mine, 8)]
                sent[which, level] = sums[which, level, pl.ds(other, 8)].astype(BF16)


def outer(steps, levels, width, left, right, coef, forward, first_sums, stair, out, state, mat, sums, wide_f):
    step = pl.program_id(0)

    @pl.when(step == 0)
    def _():
        for side in range(2):
            empty = jnp.zeros((9, 1, 24, 128), F32)
            state[side, :, pl.ds(0, 1)] = empty
            state[side, :, pl.ds(levels + 1, 1)] = empty

        def load(level, carry):
            for field in range(9):
                state[0, field, level + 1, pl.ds(FRONT, 8)] = left[field, level].astype(F32)
                state[0, field, level + 1, pl.ds(FRONT + 8, 8)] = stair[0, field, level, pl.ds(0, 8)]
                state[1, field, level + 1, pl.ds(0, 8)] = stair[1, field, level, pl.ds(8, 8)]
                state[1, field, level + 1, pl.ds(FRONT, 8)] = right[field, level].astype(F32)
                wide_f[0, field, level, pl.ds(0, 8)] = jnp.zeros((8, 128), F32)
                wide_f[1, field, level, pl.ds(8, 8)] = jnp.zeros((8, 128), F32)
            for which in range(3):
                mat[0, which, level, pl.ds(0, 8)] = left[9 + which, level].astype(F32)
                mat[0, which, level, pl.ds(8, 16)] = coef[which, level, pl.ds(0, 16)]
                mat[1, which, level, pl.ds(0, 16)] = coef[which, level, pl.ds(width - 16, 16)]
                mat[1, which, level, pl.ds(16, 8)] = right[9 + which, level].astype(F32)
                for side in range(2):
                    sums[side, which, level] = jnp.zeros((24, 128), F32)
            return carry

        lax.fori_loop(0, levels, load, 0)

    def widen(level):
        for field in range(9):
            wide_f[0, field, level, pl.ds(8, 8)] = forward[step, field, level, pl.ds(0, 16)].astype(F32)[:8]
            wide_f[1, field, level, pl.ds(0, 8)] = forward[step, field, level, pl.ds(width - 16, 16)].astype(F32)[8:]

    for level in range(levels):
        widen(level)

    old_x, new_x, old_s = (0, -1), (-1, 0), (1, -1)
    x_coef, s_coef, f_row = (step, 15 - step), (step + 1, 15 - step), (step + 1, 7 - step)

    def velocity(level):
        for side in range(2):

            def at(field, lev, lon):
                return state[side, field, level + 1 + lev, pl.ds(FRONT + old_x[side] + lon, 8)]

            def put(field, lon, value):
                state[side, field, level + 1, pl.ds(FRONT + new_x[side] + lon, 8)] = value

            x_buoy = mat[side, BUOY, level, pl.ds(x_coef[side], 8)]
            yz_buoy = mat[side, BUOY, level, pl.ds(x_coef[side] + 1, 8)]
            push(at, put, (x_buoy, 1, yz_buoy))
        for field in (VX, VY, VZ):
            first, row = (step, 7) if field == VX else (step + 1, 8)
            state[0, field, level + 1, pl.ds(FRONT + row, 1)] = stair[0, field, level, pl.ds(first, 1)]
            last, row = (14 - step, -1) if field == VX else (15 - step, 0)
            state[1, field, level + 1, pl.ds(FRONT + row, 1)] = stair[1, field, level, pl.ds(last, 1)]

    def stress(level):
        for side in range(2):

            def at(field, lev, lon):
                row = FRONT + lon + (old_s[side] if field >= 3 else 0)
                return state[side, field, level + 1 + lev, pl.ds(row, 8)]

            def put(field, lon, value):
                state[side, field, level + 1, pl.ds(FRONT + lon, 8)] = value

            rows = pl.ds(s_coef[side], 8)
            parts = strain(at, put, mat[side, LAME, level, rows], mat[side, SHEAR2, level, rows])
            f = [wide_f[side, field, level, pl.ds(f_row[side], 8)] for field in range(9)]
            for which, term in enumerate(terms(*parts, f)):
                before = sums[side, which, level, pl.ds(8 + old_s[side], 8)]
                sums[side, which, level, pl.ds(8, 8)] = before + term
        for field in range(3, 9):
            state[0, field, level + 1, pl.ds(FRONT + 8, 1)] = stair[0, field, level, pl.ds(step + 1, 1)]
            state[1, field, level + 1, pl.ds(FRONT - 1, 1)] = stair[1, field, level, pl.ds(14 - step, 1)]

    velocity(0)
    for level in range(levels):
        if level + 1 < levels:
            velocity(level + 1)
        stress(level)

    @pl.when(step == steps - 1)
    def _():
        for level in range(levels):
            for which in range(3):
                for side, start in enumerate((0, width - 8)):
                    out[side, which, level] = sums[side, which, level, pl.ds(8, 8)] + first_sums[which, level, pl.ds(start, 8)]


def prepare(levels, width, row, init_hbm, material, first, last, init, coef, own, arrived):
    copy = pltpu.make_async_copy(init_hbm, init, arrived.at[0])
    copy.start()

    def materials(level, carry):
        p, s, rho = [material[which, level] for which in range(3)]
        parts = (rho * (p * p - 2.0 * s * s), 2.0 * rho * s * s, 1.0 / rho)
        for which, part in enumerate(parts):
            coef[which, level] = part
            first[9 + which, level] = part[:HALO].astype(BF16)
            last[9 + which, level] = part[width - HALO :].astype(BF16)
        return carry

    lax.fori_loop(0, levels, materials, 0, unroll=4)
    for which in range(3):
        own[which] = material[which, row[0]]
    copy.wait()

    def edges(level, carry):
        for field in range(9):
            first[field, level] = init[field, level, pl.ds(0, 16)].astype(F32)[:HALO].astype(BF16)
            last[field, level] = init[field, level, pl.ds(width - 16, 16)].astype(F32)[16 - HALO :].astype(BF16)
        return carry

    lax.fori_loop(0, levels, edges, 0, unroll=4)


def join(levels, ends, kept, swapped, out):
    for level in range(levels):
        for which, factor in enumerate((1.0, 2.0, 1.0)):
            quarter = kept[which, level] + swapped[which, level].astype(F32)
            both = [ends[side, which, level] for side in range(2)]
            out[level, which] = (factor * jnp.concatenate(both + [quarter])).astype(BF16)


def finish(events, parts, own, out):
    def summed(which, first, last):
        total = parts[first, which].astype(F32)
        for event in range(first + 1, last):
            total = total + parts[event, which].astype(F32)
        return total

    half = events // 2
    total = []
    for which in range(3):
        low, high = summed(which, 0, half), summed(which, half, events)
        ends = low[:16] + high[:16]
        total.append(jnp.concatenate([ends[:8], low[16:], high[16:], ends[8:]]))
    p_speed, s_speed, density = own[0], own[1], own[2]
    lame = density * (p_speed * p_speed - 2.0 * s_speed * s_speed)
    shear = density * s_speed * s_speed
    out[0, 0] = 2.0 * density * p_speed * p_speed * total[0]
    out[1, 0] = 2.0 * density * s_speed * s_speed * (total[1] - 2.0 * total[0])
    out[2, 0] = density * total[2] + lame * total[0] + shear * total[1]


IN_VMEM = pl.BlockSpec(memory_space=pltpu.VMEM)
IN_HBM = pl.BlockSpec(memory_space=pltpu.HBM)
MEBI = 1024 * 1024


def run_prepare(row, init, material):
    _, levels, width, lat = init.shape
    edge = jax.ShapeDtypeStruct((12, levels, HALO, lat), BF16)
    return pl.pallas_call(
        functools.partial(prepare, levels, width),
        in_specs=[pl.BlockSpec(memory_space=pltpu.SMEM)] + [IN_HBM, IN_VMEM],
        out_specs=[IN_VMEM] * 5,
        out_shape=[
            edge,
            edge,
            jax.ShapeDtypeStruct(init.shape, BF16),
            jax.ShapeDtypeStruct((3, levels, width, lat), F32),
            jax.ShapeDtypeStruct((3, width, lat), F32),
        ],
        scratch_shapes=[pltpu.SemaphoreType.DMA((1,))],
        compiler_params=pltpu.CompilerParams(vmem_limit_bytes=50 * MEBI),
    )(row, init, material)


def run_join(ends, kept, swapped):
    _, levels, _, lat = kept.shape
    return pl.pallas_call(
        functools.partial(join, levels),
        in_specs=[IN_VMEM] * 3,
        out_specs=IN_VMEM,
        out_shape=jax.ShapeDtypeStruct((levels, 3, 24, lat), BF16),
        compiler_params=pltpu.CompilerParams(vmem_limit_bytes=8 * MEBI),
    )(ends, kept, swapped)


def run_finish(parts, own):
    events, _, _, lat = parts.shape
    width = own.shape[1]
    return pl.pallas_call(
        functools.partial(finish, events),
        in_specs=[IN_VMEM] * 2,
        out_specs=IN_VMEM,
        out_shape=jax.ShapeDtypeStruct((3, 1, width, lat), F32),
        compiler_params=pltpu.CompilerParams(vmem_limit_bytes=8 * MEBI),
    )(parts, own)


def run_inner(half, init, coef, forward):
    _, steps, _, levels, width, lat = forward.shape
    outs = [
        jax.ShapeDtypeStruct((3, levels, width, lat), F32),
        jax.ShapeDtypeStruct((3, levels, 8, lat), BF16),
        jax.ShapeDtypeStruct((3, levels, 8, lat), F32),
        jax.ShapeDtypeStruct((2, 9, levels, 16, lat), F32),
        jax.ShapeDtypeStruct(forward.shape[1:], BF16),
    ]
    return pl.pallas_call(
        functools.partial(inner, steps, levels, width),
        grid=(steps,),
        in_specs=[pl.BlockSpec(memory_space=pltpu.SMEM), IN_VMEM, IN_VMEM, IN_HBM],
        out_specs=[IN_VMEM] * 5,
        out_shape=outs,
        scratch_shapes=[
            pltpu.VMEM((9, levels + 2, width + 2 * PAD, lat), F32),
            pltpu.SemaphoreType.DMA((steps,)),
        ],
        compiler_params=pltpu.CompilerParams(vmem_limit_bytes=34 * MEBI),
        cost_estimate=pl.CostEstimate(flops=60_000_000, bytes_accessed=30_000_000, transcendentals=0),
    )(half, init, coef, forward)


def run_outer(left, right, coef, forward, first_sums, stair):
    steps, _, levels, width, lat = forward.shape
    return pl.pallas_call(
        functools.partial(outer, steps, levels, width),
        grid=(steps,),
        in_specs=[IN_VMEM] * 6,
        out_specs=IN_VMEM,
        out_shape=jax.ShapeDtypeStruct((2, 3, levels, 8, lat), F32),
        scratch_shapes=[
            pltpu.VMEM((2, 9, levels + 2, 24, lat), F32),
            pltpu.VMEM((2, 3, levels, 24, lat), F32),
            pltpu.VMEM((2, 3, levels, 24, lat), F32),
            pltpu.VMEM((2, 9, levels, 16, lat), F32),
        ],
        compiler_params=pltpu.CompilerParams(vmem_limit_bytes=34 * MEBI),
        cost_estimate=pl.CostEstimate(flops=30_000_000, bytes_accessed=20_000_000, transcendentals=0),
    )(left, right, coef, forward, first_sums, stair)


def shards(adjoint_init, forward_state, p_speed, s_speed, density):
    init = adjoint_init[0]
    row = lax.axis_index("event").reshape(1)
    first, last, init, coef, own = run_prepare(row, init, jnp.stack([p_speed, s_speed, density]))
    count = lax.axis_size("lon")
    up = [(i, (i + 1) % count) for i in range(count)]
    left = lax.ppermute(last, "lon", up)
    right = lax.ppermute(first, "lon", [(j, i) for i, j in up])
    pairs = lax.axis_size("event") // 2
    first_sums, sent, kept, stair, forward = run_inner(row // pairs, init, coef, forward_state)
    swap = [(i, (i + pairs) % (2 * pairs)) for i in range(2 * pairs)]
    swapped = lax.ppermute(sent, "event", swap)
    ends = run_outer(left, right, coef, forward, first_sums, stair)
    partial = run_join(ends, kept, swapped)
    parts = lax.all_to_all(partial, "event", 0, 0, tiled=True)
    return run_finish(parts, own)


def solution(mesh):
    placed = (
        P("event", None, None, "lon", None),
        P("event", None, None, None, "lon", None),
        P(None, "lon", None),
        P(None, "lon", None),
        P(None, "lon", None),
    )
    return jax.shard_map(
        shards, mesh=mesh, in_specs=placed, out_specs=P(None, "event", "lon", None), check_vma=False
    )
```

```python
import functools

import jax
import jax.numpy as jnp
from jax import lax
from jax.experimental import pallas as pl
from jax.experimental.pallas import tpu as pltpu
from jax.sharding import PartitionSpec as P

F32, BF16 = jnp.float32, jnp.bfloat16
HALO = 8
PAD = 8
FRONT = 8
VX, VY, VZ, XX, YY, ZZ, XY, XZ, YZ = range(9)
LAME, SHEAR2, BUOY = range(3)


def before_lat(value):
    edge = lax.broadcasted_iota(jnp.int32, value.shape, 1) == 0
    return jnp.where(edge, 0.0, pltpu.roll(value, 1, 1))


def after_lat(value):
    edge = lax.broadcasted_iota(jnp.int32, value.shape, 1) == 127
    return jnp.where(edge, 0.0, pltpu.roll(value, 127, 1))


def rounded(value):
    return value.astype(BF16).astype(F32)


def push(at, put, buoy):
    x_buoy, shift, yz_buoy = buoy
    xy, xz = at(XY, 0, shift), at(XZ, 0, shift)
    xy_x, xz_x = at(XY, 0, 0), at(XZ, 0, 0)
    yz = at(YZ, 0, shift)
    force_x = (at(XX, 0, 1) - at(XX, 0, 0)) + (xy_x - before_lat(xy_x)) + (xz_x - at(XZ, -1, 0))
    yy = at(YY, 0, shift)
    force_y = (xy - at(XY, 0, shift - 1)) + (after_lat(yy) - yy) + (yz - at(YZ, -1, shift))
    force_z = (
        (xz - at(XZ, 0, shift - 1))
        + (yz - before_lat(yz))
        + (at(ZZ, 1, shift) - at(ZZ, 0, shift))
    )
    put(VX, 0, rounded(at(VX, 0, 0) + x_buoy * force_x))
    put(VY, shift, rounded(at(VY, 0, shift) + yz_buoy * force_y))
    put(VZ, shift, rounded(at(VZ, 0, shift) + yz_buoy * force_z))


def strain(at, put, lame, shear2):
    vx, vy, vz = at(VX, 0, 0), at(VY, 0, 0), at(VZ, 0, 0)
    e_xx = vx - at(VX, 0, -1)
    e_yy = vy - before_lat(vy)
    e_zz = vz - at(VZ, -1, 0)
    d_xy = (after_lat(vx) - vx) + (at(VY, 0, 1) - vy)
    d_xz = (at(VX, 1, 0) - vx) + (at(VZ, 0, 1) - vz)
    d_yz = (at(VY, 1, 0) - vy) + (after_lat(vz) - vz)
    trace = e_xx + e_yy + e_zz
    shear = 0.5 * shear2
    volume = lame * trace
    for field, change in (
        (XX, volume + shear2 * e_xx),
        (YY, volume + shear2 * e_yy),
        (ZZ, volume + shear2 * e_zz),
        (XY, shear * d_xy),
        (XZ, shear * d_xz),
        (YZ, shear * d_yz),
    ):
        put(field, 0, rounded(at(field, 0, 0) + change))
    return (vx, vy, vz), (e_xx, e_yy, e_zz, d_xy, d_xz, d_yz), trace


def terms(speed, rate, trace, f):
    return (
        trace * (f[3] + f[4] + f[5]),
        (rate[0] * f[3] + rate[1] * f[4] + rate[2] * f[5])
        + (rate[3] * f[6] + rate[4] * f[7] + rate[5] * f[8]),
        speed[0] * f[0] + speed[1] * f[1] + speed[2] * f[2],
    )


def inner(steps, levels, width, half, init, coef, forward_hbm, sums, sent, kept, stair, forward, state, arrived):
    step = pl.program_id(0)

    starts = (0, 2)

    def fetch(group):
        begin = starts[group]
        part = pl.ds(begin, (starts + (steps,))[group + 1] - begin)
        return pltpu.make_async_copy(forward_hbm.at[0, part], forward.at[part], arrived.at[group])

    def keep(level, side, field, row, value):
        stair[side, field, level, pl.ds(row, 1)] = value

    @pl.when(step == 0)
    def _():
        for group in range(len(starts)):
            fetch(group).start()
        empty = jnp.zeros((9, 1, width + 2 * PAD, 128), F32)
        state[:, pl.ds(0, 1)] = empty
        state[:, pl.ds(levels + 1, 1)] = empty

        def load(level, carry):
            for field in range(9):
                state[field, level + 1, pl.ds(0, PAD)] = jnp.zeros((PAD, 128), F32)
                state[field, level + 1, pl.ds(PAD + width, PAD)] = jnp.zeros((PAD, 128), F32)
                state[field, level + 1, pl.ds(PAD, width)] = init[field, level].astype(F32)
                stair[0, field, level] = jnp.zeros((16, 128), F32)
                stair[1, field, level] = jnp.zeros((16, 128), F32)
                if field != VX:
                    stair[0, field, level, pl.ds(0, 1)] = state[field, level + 1, pl.ds(PAD, 1)]
                if field not in (VY, VZ):
                    stair[1, field, level, pl.ds(15, 1)] = state[field, level + 1, pl.ds(PAD + width - 1, 1)]
            for which in range(3):
                sums[which, level] = jnp.zeros((width, 128), F32)
            return carry

        lax.fori_loop(0, levels, load, 0)

    def view(level, start, rows):
        def at(field, lev, lon):
            return state[field, level + 1 + lev, pl.ds(PAD + start + lon, rows)]

        def put(field, lon, value):
            state[field, level + 1, pl.ds(PAD + start + lon, rows)] = value

        return at, put

    def velocity(level):
        for start in range(0, width, 16):
            buoy = coef[BUOY, level, pl.ds(start, 16)]
            push(*view(level, start, 16), (buoy, 0, buoy))
        for field in (VX, VY, VZ):
            first = step if field == VX else step + 1
            last = 30 - step if field == VX else 31 - step
            keep(level, 0, field, first, state[field, level + 1, pl.ds(PAD + first, 1)])
            keep(level, 1, field, last - 16, state[field, level + 1, pl.ds(PAD + last, 1)])

    def stress(level):
        for start in range(0, width, 16):
            mine = pl.ds(start, 16)
            parts = strain(*view(level, start, 16), coef[LAME, level, mine], coef[SHEAR2, level, mine])
            f = [forward[step, field, level, mine].astype(F32) for field in range(9)]
            column = lax.broadcasted_iota(jnp.int32, (8, 128), 0)
            for which, term in enumerate(terms(*parts, f)):
                if start == 0:
                    term = jnp.concatenate([jnp.where(column > step, term[:8], 0.0), term[8:]])
                elif start == width - 16:
                    term = jnp.concatenate([term[:8], jnp.where(column < 7 - step, term[8:], 0.0)])
                sums[which, level, mine] += term
        for field in range(3, 9):
            keep(level, 0, field, step + 1, state[field, level + 1, pl.ds(PAD + step + 1, 1)])
            keep(level, 1, field, 14 - step, state[field, level + 1, pl.ds(PAD + 30 - step, 1)])

    for group, begin in enumerate(starts):
        pl.when(step == begin)(fetch(group).wait)

    velocity(0)
    for level in range(levels):
        if level + 1 < levels:
            velocity(level + 1)
        stress(level)

    @pl.when(step == steps - 1)
    def _():
        mine = pl.multiple_of(8 + 8 * half[0], 8)
        other = pl.multiple_of(16 - 8 * half[0], 8)
        for level in range(levels):
            for which in range(3):
                kept[which, level] = sums[which, level, pl.ds(mine, 8)]
                sent[which, level] = sums[which, level, pl.ds(other, 8)].astype(BF16)


def outer(steps, levels, width, left, right, coef, forward, first_sums, stair, out, state, mat, sums, wide_f):
    step = pl.program_id(0)

    @pl.when(step == 0)
    def _():
        for side in range(2):
            empty = jnp.zeros((9, 1, 24, 128), F32)
            state[side, :, pl.ds(0, 1)] = empty
            state[side, :, pl.ds(levels + 1, 1)] = empty

        def load(level, carry):
            for field in range(9):
                state[0, field, level + 1, pl.ds(FRONT, 8)] = left[field, level].astype(F32)
                state[0, field, level + 1, pl.ds(FRONT + 8, 8)] = stair[0, field, level, pl.ds(0, 8)]
                state[1, field, level + 1, pl.ds(0, 8)] = stair[1, field, level, pl.ds(8, 8)]
                state[1, field, level + 1, pl.ds(FRONT, 8)] = right[field, level].astype(F32)
                wide_f[0, field, level, pl.ds(0, 8)] = jnp.zeros((8, 128), F32)
                wide_f[1, field, level, pl.ds(8, 8)] = jnp.zeros((8, 128), F32)
            for which in range(3):
                mat[0, which, level, pl.ds(0, 8)] = left[9 + which, level].astype(F32)
                mat[0, which, level, pl.ds(8, 16)] = coef[which, level, pl.ds(0, 16)]
                mat[1, which, level, pl.ds(0, 16)] = coef[which, level, pl.ds(width - 16, 16)]
                mat[1, which, level, pl.ds(16, 8)] = right[9 + which, level].astype(F32)
                for side in range(2):
                    sums[side, which, level] = jnp.zeros((24, 128), F32)
            return carry

        lax.fori_loop(0, levels, load, 0)

    def widen(level):
        for field in range(9):
            wide_f[0, field, level, pl.ds(8, 8)] = forward[step, field, level, pl.ds(0, 16)].astype(F32)[:8]
            wide_f[1, field, level, pl.ds(0, 8)] = forward[step, field, level, pl.ds(width - 16, 16)].astype(F32)[8:]

    for level in range(levels):
        widen(level)

    old_x, new_x, old_s = (0, -1), (-1, 0), (1, -1)
    x_coef, s_coef, f_row = (step, 15 - step), (step + 1, 15 - step), (step + 1, 7 - step)

    def velocity(level):
        for side in range(2):

            def at(field, lev, lon):
                return state[side, field, level + 1 + lev, pl.ds(FRONT + old_x[side] + lon, 8)]

            def put(field, lon, value):
                state[side, field, level + 1, pl.ds(FRONT + new_x[side] + lon, 8)] = value

            x_buoy = mat[side, BUOY, level, pl.ds(x_coef[side], 8)]
            yz_buoy = mat[side, BUOY, level, pl.ds(x_coef[side] + 1, 8)]
            push(at, put, (x_buoy, 1, yz_buoy))
        for field in (VX, VY, VZ):
            first, row = (step, 7) if field == VX else (step + 1, 8)
            state[0, field, level + 1, pl.ds(FRONT + row, 1)] = stair[0, field, level, pl.ds(first, 1)]
            last, row = (14 - step, -1) if field == VX else (15 - step, 0)
            state[1, field, level + 1, pl.ds(FRONT + row, 1)] = stair[1, field, level, pl.ds(last, 1)]

    def stress(level):
        for side in range(2):

            def at(field, lev, lon):
                row = FRONT + lon + (old_s[side] if field >= 3 else 0)
                return state[side, field, level + 1 + lev, pl.ds(row, 8)]

            def put(field, lon, value):
                state[side, field, level + 1, pl.ds(FRONT + lon, 8)] = value

            rows = pl.ds(s_coef[side], 8)
            parts = strain(at, put, mat[side, LAME, level, rows], mat[side, SHEAR2, level, rows])
            f = [wide_f[side, field, level, pl.ds(f_row[side], 8)] for field in range(9)]
            for which, term in enumerate(terms(*parts, f)):
                before = sums[side, which, level, pl.ds(8 + old_s[side], 8)]
                sums[side, which, level, pl.ds(8, 8)] = before + term
        for field in range(3, 9):
            state[0, field, level + 1, pl.ds(FRONT + 8, 1)] = stair[0, field, level, pl.ds(step + 1, 1)]
            state[1, field, level + 1, pl.ds(FRONT - 1, 1)] = stair[1, field, level, pl.ds(14 - step, 1)]

    velocity(0)
    for level in range(levels):
        if level + 1 < levels:
            velocity(level + 1)
        stress(level)

    @pl.when(step == steps - 1)
    def _():
        for level in range(levels):
            for which in range(3):
                for side, start in enumerate((0, width - 8)):
                    out[side, which, level] = sums[side, which, level, pl.ds(8, 8)] + first_sums[which, level, pl.ds(start, 8)]


def prepare(levels, width, row, init_hbm, material, first, last, init, coef, own, arrived):
    copy = pltpu.make_async_copy(init_hbm, init, arrived.at[0])
    copy.start()

    def materials(level, carry):
        p, s, rho = [material[which, level] for which in range(3)]
        parts = (rho * (p * p - 2.0 * s * s), 2.0 * rho * s * s, 1.0 / rho)
        for which, part in enumerate(parts):
            coef[which, level] = part
            first[9 + which, level] = part[:HALO].astype(BF16)
            last[9 + which, level] = part[width - HALO :].astype(BF16)
        return carry

    lax.fori_loop(0, levels, materials, 0, unroll=4)
    for which in range(3):
        own[which] = material[which, row[0]]
    copy.wait()

    def edges(level, carry):
        for field in range(9):
            first[field, level] = init[field, level, pl.ds(0, 16)].astype(F32)[:HALO].astype(BF16)
            last[field, level] = init[field, level, pl.ds(width - 16, 16)].astype(F32)[16 - HALO :].astype(BF16)
        return carry

    lax.fori_loop(0, levels, edges, 0, unroll=4)


def join(levels, ends, kept, swapped, out):
    for level in range(levels):
        for which, factor in enumerate((1.0, 2.0, 1.0)):
            quarter = kept[which, level] + swapped[which, level].astype(F32)
            both = [ends[side, which, level] for side in range(2)]
            out[level, which] = (factor * jnp.concatenate(both + [quarter])).astype(BF16)


def finish(events, parts, own, out):
    def summed(which, first, last):
        total = parts[first, which].astype(F32)
        for event in range(first + 1, last):
            total = total + parts[event, which].astype(F32)
        return total

    half = events // 2
    total = []
    for which in range(3):
        low, high = summed(which, 0, half), summed(which, half, events)
        ends = low[:16] + high[:16]
        total.append(jnp.concatenate([ends[:8], low[16:], high[16:], ends[8:]]))
    p_speed, s_speed, density = own[0], own[1], own[2]
    lame = density * (p_speed * p_speed - 2.0 * s_speed * s_speed)
    shear = density * s_speed * s_speed
    out[0, 0] = 2.0 * density * p_speed * p_speed * total[0]
    out[1, 0] = 2.0 * density * s_speed * s_speed * (total[1] - 2.0 * total[0])
    out[2, 0] = density * total[2] + lame * total[0] + shear * total[1]


IN_VMEM = pl.BlockSpec(memory_space=pltpu.VMEM)
IN_HBM = pl.BlockSpec(memory_space=pltpu.HBM)
MEBI = 1024 * 1024


def run_prepare(row, init, material):
    _, levels, width, lat = init.shape
    edge = jax.ShapeDtypeStruct((12, levels, HALO, lat), BF16)
    return pl.pallas_call(
        functools.partial(prepare, levels, width),
        in_specs=[pl.BlockSpec(memory_space=pltpu.SMEM)] + [IN_HBM, IN_VMEM],
        out_specs=[IN_VMEM] * 5,
        out_shape=[
            edge,
            edge,
            jax.ShapeDtypeStruct(init.shape, BF16),
            jax.ShapeDtypeStruct((3, levels, width, lat), F32),
            jax.ShapeDtypeStruct((3, width, lat), F32),
        ],
        scratch_shapes=[pltpu.SemaphoreType.DMA((1,))],
        compiler_params=pltpu.CompilerParams(vmem_limit_bytes=50 * MEBI),
    )(row, init, material)


def run_join(ends, kept, swapped):
    _, levels, _, lat = kept.shape
    return pl.pallas_call(
        functools.partial(join, levels),
        in_specs=[IN_VMEM] * 3,
        out_specs=IN_VMEM,
        out_shape=jax.ShapeDtypeStruct((levels, 3, 24, lat), BF16),
        compiler_params=pltpu.CompilerParams(vmem_limit_bytes=8 * MEBI),
    )(ends, kept, swapped)


def run_finish(parts, own):
    events, _, _, lat = parts.shape
    width = own.shape[1]
    return pl.pallas_call(
        functools.partial(finish, events),
        in_specs=[IN_VMEM] * 2,
        out_specs=IN_VMEM,
        out_shape=jax.ShapeDtypeStruct((3, 1, width, lat), F32),
        compiler_params=pltpu.CompilerParams(vmem_limit_bytes=8 * MEBI),
    )(parts, own)


def run_inner(half, init, coef, forward):
    _, steps, _, levels, width, lat = forward.shape
    outs = [
        jax.ShapeDtypeStruct((3, levels, width, lat), F32),
        jax.ShapeDtypeStruct((3, levels, 8, lat), BF16),
        jax.ShapeDtypeStruct((3, levels, 8, lat), F32),
        jax.ShapeDtypeStruct((2, 9, levels, 16, lat), F32),
        jax.ShapeDtypeStruct(forward.shape[1:], BF16),
    ]
    return pl.pallas_call(
        functools.partial(inner, steps, levels, width),
        grid=(steps,),
        in_specs=[pl.BlockSpec(memory_space=pltpu.SMEM), IN_VMEM, IN_VMEM, IN_HBM],
        out_specs=[IN_VMEM] * 5,
        out_shape=outs,
        scratch_shapes=[
            pltpu.VMEM((9, levels + 2, width + 2 * PAD, lat), F32),
            pltpu.SemaphoreType.DMA((2,)),
        ],
        compiler_params=pltpu.CompilerParams(vmem_limit_bytes=34 * MEBI),
        cost_estimate=pl.CostEstimate(flops=60_000_000, bytes_accessed=30_000_000, transcendentals=0),
    )(half, init, coef, forward)


def run_outer(left, right, coef, forward, first_sums, stair):
    steps, _, levels, width, lat = forward.shape
    return pl.pallas_call(
        functools.partial(outer, steps, levels, width),
        grid=(steps,),
        in_specs=[IN_VMEM] * 6,
        out_specs=IN_VMEM,
        out_shape=jax.ShapeDtypeStruct((2, 3, levels, 8, lat), F32),
        scratch_shapes=[
            pltpu.VMEM((2, 9, levels + 2, 24, lat), F32),
            pltpu.VMEM((2, 3, levels, 24, lat), F32),
            pltpu.VMEM((2, 3, levels, 24, lat), F32),
            pltpu.VMEM((2, 9, levels, 16, lat), F32),
        ],
        compiler_params=pltpu.CompilerParams(vmem_limit_bytes=34 * MEBI),
        cost_estimate=pl.CostEstimate(flops=30_000_000, bytes_accessed=20_000_000, transcendentals=0),
    )(left, right, coef, forward, first_sums, stair)


def shards(adjoint_init, forward_state, p_speed, s_speed, density):
    init = adjoint_init[0]
    row = lax.axis_index("event").reshape(1)
    first, last, init, coef, own = run_prepare(row, init, jnp.stack([p_speed, s_speed, density]))
    count = lax.axis_size("lon")
    up = [(i, (i + 1) % count) for i in range(count)]
    left = lax.ppermute(last, "lon", up)
    right = lax.ppermute(first, "lon", [(j, i) for i, j in up])
    pairs = lax.axis_size("event") // 2
    first_sums, sent, kept, stair, forward = run_inner(row // pairs, init, coef, forward_state)
    swap = [(i, (i + pairs) % (2 * pairs)) for i in range(2 * pairs)]
    swapped = lax.ppermute(sent, "event", swap)
    ends = run_outer(left, right, coef, forward, first_sums, stair)
    partial = run_join(ends, kept, swapped)
    parts = lax.all_to_all(partial, "event", 0, 0, tiled=True)
    return run_finish(parts, own)


def solution(mesh):
    placed = (
        P("event", None, None, "lon", None),
        P("event", None, None, None, "lon", None),
        P(None, "lon", None),
        P(None, "lon", None),
        P(None, "lon", None),
    )
    return jax.shard_map(
        shards, mesh=mesh, in_specs=placed, out_specs=P(None, "event", "lon", None), check_vma=False
    )
```

```python
import functools

import jax
import jax.numpy as jnp
from jax import lax
from jax.experimental import pallas as pl
from jax.experimental.pallas import tpu as pltpu
from jax.sharding import PartitionSpec as P

F32, BF16 = jnp.float32, jnp.bfloat16
HALO = 8
PAD = 8
FRONT = 8
VX, VY, VZ, XX, YY, ZZ, XY, XZ, YZ = range(9)
LAME, SHEAR2, BUOY = range(3)


def before_lat(value):
    edge = lax.broadcasted_iota(jnp.int32, value.shape, 1) == 0
    return jnp.where(edge, 0.0, pltpu.roll(value, 1, 1))


def after_lat(value):
    edge = lax.broadcasted_iota(jnp.int32, value.shape, 1) == 127
    return jnp.where(edge, 0.0, pltpu.roll(value, 127, 1))


def rounded(value):
    return value.astype(BF16).astype(F32)


def push(at, put, buoy):
    x_buoy, shift, yz_buoy = buoy
    xy, xz = at(XY, 0, shift), at(XZ, 0, shift)
    xy_x, xz_x = at(XY, 0, 0), at(XZ, 0, 0)
    yz = at(YZ, 0, shift)
    force_x = (at(XX, 0, 1) - at(XX, 0, 0)) + (xy_x - before_lat(xy_x)) + (xz_x - at(XZ, -1, 0))
    yy = at(YY, 0, shift)
    force_y = (xy - at(XY, 0, shift - 1)) + (after_lat(yy) - yy) + (yz - at(YZ, -1, shift))
    force_z = (
        (xz - at(XZ, 0, shift - 1))
        + (yz - before_lat(yz))
        + (at(ZZ, 1, shift) - at(ZZ, 0, shift))
    )
    put(VX, 0, rounded(at(VX, 0, 0) + x_buoy * force_x))
    put(VY, shift, rounded(at(VY, 0, shift) + yz_buoy * force_y))
    put(VZ, shift, rounded(at(VZ, 0, shift) + yz_buoy * force_z))


def strain(at, put, lame, shear2):
    vx, vy, vz = at(VX, 0, 0), at(VY, 0, 0), at(VZ, 0, 0)
    e_xx = vx - at(VX, 0, -1)
    e_yy = vy - before_lat(vy)
    e_zz = vz - at(VZ, -1, 0)
    d_xy = (after_lat(vx) - vx) + (at(VY, 0, 1) - vy)
    d_xz = (at(VX, 1, 0) - vx) + (at(VZ, 0, 1) - vz)
    d_yz = (at(VY, 1, 0) - vy) + (after_lat(vz) - vz)
    trace = e_xx + e_yy + e_zz
    shear = 0.5 * shear2
    volume = lame * trace
    for field, change in (
        (XX, volume + shear2 * e_xx),
        (YY, volume + shear2 * e_yy),
        (ZZ, volume + shear2 * e_zz),
        (XY, shear * d_xy),
        (XZ, shear * d_xz),
        (YZ, shear * d_yz),
    ):
        put(field, 0, rounded(at(field, 0, 0) + change))
    return (vx, vy, vz), (e_xx, e_yy, e_zz, d_xy, d_xz, d_yz), trace


def terms(speed, rate, trace, f):
    return (
        trace * (f[3] + f[4] + f[5]),
        (rate[0] * f[3] + rate[1] * f[4] + rate[2] * f[5])
        + (rate[3] * f[6] + rate[4] * f[7] + rate[5] * f[8]),
        speed[0] * f[0] + speed[1] * f[1] + speed[2] * f[2],
    )


def inner(steps, levels, width, half, init, coef, forward_hbm, sums, sent, kept, stair, forward, state, arrived):
    step = pl.program_id(0)

    starts = (0, 1, 3)

    def fetch(group):
        begin = starts[group]
        part = pl.ds(begin, (starts + (steps,))[group + 1] - begin)
        return pltpu.make_async_copy(forward_hbm.at[0, part], forward.at[part], arrived.at[group])

    def keep(level, side, field, row, value):
        stair[side, field, level, pl.ds(row, 1)] = value

    @pl.when(step == 0)
    def _():
        fetch(0).start()
        empty = jnp.zeros((9, 1, width + 2 * PAD, 128), F32)
        state[:, pl.ds(0, 1)] = empty
        state[:, pl.ds(levels + 1, 1)] = empty

        def load(level, carry):
            for field in range(9):
                state[field, level + 1, pl.ds(0, PAD)] = jnp.zeros((PAD, 128), F32)
                state[field, level + 1, pl.ds(PAD + width, PAD)] = jnp.zeros((PAD, 128), F32)
                state[field, level + 1, pl.ds(PAD, width)] = init[field, level].astype(F32)
                stair[0, field, level] = jnp.zeros((16, 128), F32)
                stair[1, field, level] = jnp.zeros((16, 128), F32)
                if field != VX:
                    stair[0, field, level, pl.ds(0, 1)] = state[field, level + 1, pl.ds(PAD, 1)]
                if field not in (VY, VZ):
                    stair[1, field, level, pl.ds(15, 1)] = state[field, level + 1, pl.ds(PAD + width - 1, 1)]
            for which in range(3):
                sums[which, level] = jnp.zeros((width, 128), F32)
            return carry

        lax.fori_loop(0, levels, load, 0)
        for group in range(1, len(starts)):
            fetch(group).start()

    def view(level, start, rows):
        def at(field, lev, lon):
            return state[field, level + 1 + lev, pl.ds(PAD + start + lon, rows)]

        def put(field, lon, value):
            state[field, level + 1, pl.ds(PAD + start + lon, rows)] = value

        return at, put

    def velocity(level):
        for start in range(0, width, 16):
            buoy = coef[BUOY, level, pl.ds(start, 16)]
            push(*view(level, start, 16), (buoy, 0, buoy))
        for field in (VX, VY, VZ):
            first = step if field == VX else step + 1
            last = 30 - step if field == VX else 31 - step
            keep(level, 0, field, first, state[field, level + 1, pl.ds(PAD + first, 1)])
            keep(level, 1, field, last - 16, state[field, level + 1, pl.ds(PAD + last, 1)])

    def stress(level):
        for start in range(0, width, 16):
            mine = pl.ds(start, 16)
            parts = strain(*view(level, start, 16), coef[LAME, level, mine], coef[SHEAR2, level, mine])
            f = [forward[step, field, level, mine].astype(F32) for field in range(9)]
            column = lax.broadcasted_iota(jnp.int32, (8, 128), 0)
            for which, term in enumerate(terms(*parts, f)):
                if start == 0:
                    term = jnp.concatenate([jnp.where(column > step, term[:8], 0.0), term[8:]])
                elif start == width - 16:
                    term = jnp.concatenate([term[:8], jnp.where(column < 7 - step, term[8:], 0.0)])
                sums[which, level, mine] += term
        for field in range(3, 9):
            keep(level, 0, field, step + 1, state[field, level + 1, pl.ds(PAD + step + 1, 1)])
            keep(level, 1, field, 14 - step, state[field, level + 1, pl.ds(PAD + 30 - step, 1)])

    for group, begin in enumerate(starts):
        pl.when(step == begin)(fetch(group).wait)

    velocity(0)
    for level in range(levels):
        if level + 1 < levels:
            velocity(level + 1)
        stress(level)

    @pl.when(step == steps - 1)
    def _():
        mine = pl.multiple_of(8 + 8 * half[0], 8)
        other = pl.multiple_of(16 - 8 * half[0], 8)
        for level in range(levels):
            for which in range(3):
                kept[which, level] = sums[which, level, pl.ds(mine, 8)]
                sent[which, level] = sums[which, level, pl.ds(other, 8)].astype(BF16)


def outer(steps, levels, width, left, right, coef, forward, first_sums, stair, out, state, mat, sums, wide_f):
    step = pl.program_id(0)

    @pl.when(step == 0)
    def _():
        for side in range(2):
            empty = jnp.zeros((9, 1, 24, 128), F32)
            state[side, :, pl.ds(0, 1)] = empty
            state[side, :, pl.ds(levels + 1, 1)] = empty

        def load(level, carry):
            for field in range(9):
                state[0, field, level + 1, pl.ds(FRONT, 8)] = left[field, level].astype(F32)
                state[0, field, level + 1, pl.ds(FRONT + 8, 8)] = stair[0, field, level, pl.ds(0, 8)]
                state[1, field, level + 1, pl.ds(0, 8)] = stair[1, field, level, pl.ds(8, 8)]
                state[1, field, level + 1, pl.ds(FRONT, 8)] = right[field, level].astype(F32)
                wide_f[0, field, level, pl.ds(0, 8)] = jnp.zeros((8, 128), F32)
                wide_f[1, field, level, pl.ds(8, 8)] = jnp.zeros((8, 128), F32)
            for which in range(3):
                mat[0, which, level, pl.ds(0, 8)] = left[9 + which, level].astype(F32)
                mat[0, which, level, pl.ds(8, 16)] = coef[which, level, pl.ds(0, 16)]
                mat[1, which, level, pl.ds(0, 16)] = coef[which, level, pl.ds(width - 16, 16)]
                mat[1, which, level, pl.ds(16, 8)] = right[9 + which, level].astype(F32)
                for side in range(2):
                    sums[side, which, level] = jnp.zeros((24, 128), F32)
            return carry

        lax.fori_loop(0, levels, load, 0)

    def widen(level):
        for field in range(9):
            wide_f[0, field, level, pl.ds(8, 8)] = forward[step, field, level, pl.ds(0, 16)].astype(F32)[:8]
            wide_f[1, field, level, pl.ds(0, 8)] = forward[step, field, level, pl.ds(width - 16, 16)].astype(F32)[8:]

    for level in range(levels):
        widen(level)

    old_x, new_x, old_s = (0, -1), (-1, 0), (1, -1)
    x_coef, s_coef, f_row = (step, 15 - step), (step + 1, 15 - step), (step + 1, 7 - step)

    def velocity(level):
        for side in range(2):

            def at(field, lev, lon):
                return state[side, field, level + 1 + lev, pl.ds(FRONT + old_x[side] + lon, 8)]

            def put(field, lon, value):
                state[side, field, level + 1, pl.ds(FRONT + new_x[side] + lon, 8)] = value

            x_buoy = mat[side, BUOY, level, pl.ds(x_coef[side], 8)]
            yz_buoy = mat[side, BUOY, level, pl.ds(x_coef[side] + 1, 8)]
            push(at, put, (x_buoy, 1, yz_buoy))
        for field in (VX, VY, VZ):
            first, row = (step, 7) if field == VX else (step + 1, 8)
            state[0, field, level + 1, pl.ds(FRONT + row, 1)] = stair[0, field, level, pl.ds(first, 1)]
            last, row = (14 - step, -1) if field == VX else (15 - step, 0)
            state[1, field, level + 1, pl.ds(FRONT + row, 1)] = stair[1, field, level, pl.ds(last, 1)]

    def stress(level):
        for side in range(2):

            def at(field, lev, lon):
                row = FRONT + lon + (old_s[side] if field >= 3 else 0)
                return state[side, field, level + 1 + lev, pl.ds(row, 8)]

            def put(field, lon, value):
                state[side, field, level + 1, pl.ds(FRONT + lon, 8)] = value

            rows = pl.ds(s_coef[side], 8)
            parts = strain(at, put, mat[side, LAME, level, rows], mat[side, SHEAR2, level, rows])
            f = [wide_f[side, field, level, pl.ds(f_row[side], 8)] for field in range(9)]
            for which, term in enumerate(terms(*parts, f)):
                before = sums[side, which, level, pl.ds(8 + old_s[side], 8)]
                sums[side, which, level, pl.ds(8, 8)] = before + term
        for field in range(3, 9):
            state[0, field, level + 1, pl.ds(FRONT + 8, 1)] = stair[0, field, level, pl.ds(step + 1, 1)]
            state[1, field, level + 1, pl.ds(FRONT - 1, 1)] = stair[1, field, level, pl.ds(14 - step, 1)]

    velocity(0)
    for level in range(levels):
        if level + 1 < levels:
            velocity(level + 1)
        stress(level)

    @pl.when(step == steps - 1)
    def _():
        for level in range(levels):
            for which in range(3):
                for side, start in enumerate((0, width - 8)):
                    out[side, which, level] = sums[side, which, level, pl.ds(8, 8)] + first_sums[which, level, pl.ds(start, 8)]


def prepare(levels, width, row, init_hbm, material, first, last, init, coef, own, arrived):
    copy = pltpu.make_async_copy(init_hbm, init, arrived.at[0])
    copy.start()

    def materials(level, carry):
        p, s, rho = [material[which, level] for which in range(3)]
        parts = (rho * (p * p - 2.0 * s * s), 2.0 * rho * s * s, 1.0 / rho)
        for which, part in enumerate(parts):
            coef[which, level] = part
            first[9 + which, level] = part[:HALO].astype(BF16)
            last[9 + which, level] = part[width - HALO :].astype(BF16)
        return carry

    lax.fori_loop(0, levels, materials, 0, unroll=4)
    for which in range(3):
        own[which] = material[which, row[0]]
    copy.wait()

    def edges(level, carry):
        for field in range(9):
            first[field, level] = init[field, level, pl.ds(0, 16)].astype(F32)[:HALO].astype(BF16)
            last[field, level] = init[field, level, pl.ds(width - 16, 16)].astype(F32)[16 - HALO :].astype(BF16)
        return carry

    lax.fori_loop(0, levels, edges, 0, unroll=4)


def join(levels, ends, kept, swapped, out):
    for level in range(levels):
        for which, factor in enumerate((1.0, 2.0, 1.0)):
            quarter = kept[which, level] + swapped[which, level].astype(F32)
            both = [ends[side, which, level] for side in range(2)]
            out[level, which] = (factor * jnp.concatenate(both + [quarter])).astype(BF16)


def finish(events, parts, own, out):
    def summed(which, first, last):
        total = parts[first, which].astype(F32)
        for event in range(first + 1, last):
            total = total + parts[event, which].astype(F32)
        return total

    half = events // 2
    total = []
    for which in range(3):
        low, high = summed(which, 0, half), summed(which, half, events)
        ends = low[:16] + high[:16]
        total.append(jnp.concatenate([ends[:8], low[16:], high[16:], ends[8:]]))
    p_speed, s_speed, density = own[0], own[1], own[2]
    lame = density * (p_speed * p_speed - 2.0 * s_speed * s_speed)
    shear = density * s_speed * s_speed
    out[0, 0] = 2.0 * density * p_speed * p_speed * total[0]
    out[1, 0] = 2.0 * density * s_speed * s_speed * (total[1] - 2.0 * total[0])
    out[2, 0] = density * total[2] + lame * total[0] + shear * total[1]


IN_VMEM = pl.BlockSpec(memory_space=pltpu.VMEM)
IN_HBM = pl.BlockSpec(memory_space=pltpu.HBM)
MEBI = 1024 * 1024


def run_prepare(row, init, material):
    _, levels, width, lat = init.shape
    edge = jax.ShapeDtypeStruct((12, levels, HALO, lat), BF16)
    return pl.pallas_call(
        functools.partial(prepare, levels, width),
        in_specs=[pl.BlockSpec(memory_space=pltpu.SMEM)] + [IN_HBM, IN_VMEM],
        out_specs=[IN_VMEM] * 5,
        out_shape=[
            edge,
            edge,
            jax.ShapeDtypeStruct(init.shape, BF16),
            jax.ShapeDtypeStruct((3, levels, width, lat), F32),
            jax.ShapeDtypeStruct((3, width, lat), F32),
        ],
        scratch_shapes=[pltpu.SemaphoreType.DMA((1,))],
        compiler_params=pltpu.CompilerParams(vmem_limit_bytes=50 * MEBI),
    )(row, init, material)


def run_join(ends, kept, swapped):
    _, levels, _, lat = kept.shape
    return pl.pallas_call(
        functools.partial(join, levels),
        in_specs=[IN_VMEM] * 3,
        out_specs=IN_VMEM,
        out_shape=jax.ShapeDtypeStruct((levels, 3, 24, lat), BF16),
        compiler_params=pltpu.CompilerParams(vmem_limit_bytes=8 * MEBI),
    )(ends, kept, swapped)


def run_finish(parts, own):
    events, _, _, lat = parts.shape
    width = own.shape[1]
    return pl.pallas_call(
        functools.partial(finish, events),
        in_specs=[IN_VMEM] * 2,
        out_specs=IN_VMEM,
        out_shape=jax.ShapeDtypeStruct((3, 1, width, lat), F32),
        compiler_params=pltpu.CompilerParams(vmem_limit_bytes=8 * MEBI),
    )(parts, own)


def run_inner(half, init, coef, forward):
    _, steps, _, levels, width, lat = forward.shape
    outs = [
        jax.ShapeDtypeStruct((3, levels, width, lat), F32),
        jax.ShapeDtypeStruct((3, levels, 8, lat), BF16),
        jax.ShapeDtypeStruct((3, levels, 8, lat), F32),
        jax.ShapeDtypeStruct((2, 9, levels, 16, lat), F32),
        jax.ShapeDtypeStruct(forward.shape[1:], BF16),
    ]
    return pl.pallas_call(
        functools.partial(inner, steps, levels, width),
        grid=(steps,),
        in_specs=[pl.BlockSpec(memory_space=pltpu.SMEM), IN_VMEM, IN_VMEM, IN_HBM],
        out_specs=[IN_VMEM] * 5,
        out_shape=outs,
        scratch_shapes=[
            pltpu.VMEM((9, levels + 2, width + 2 * PAD, lat), F32),
            pltpu.SemaphoreType.DMA((3,)),
        ],
        compiler_params=pltpu.CompilerParams(vmem_limit_bytes=34 * MEBI),
        cost_estimate=pl.CostEstimate(flops=60_000_000, bytes_accessed=30_000_000, transcendentals=0),
    )(half, init, coef, forward)


def run_outer(left, right, coef, forward, first_sums, stair):
    steps, _, levels, width, lat = forward.shape
    return pl.pallas_call(
        functools.partial(outer, steps, levels, width),
        grid=(steps,),
        in_specs=[IN_VMEM] * 6,
        out_specs=IN_VMEM,
        out_shape=jax.ShapeDtypeStruct((2, 3, levels, 8, lat), F32),
        scratch_shapes=[
            pltpu.VMEM((2, 9, levels + 2, 24, lat), F32),
            pltpu.VMEM((2, 3, levels, 24, lat), F32),
            pltpu.VMEM((2, 3, levels, 24, lat), F32),
            pltpu.VMEM((2, 9, levels, 16, lat), F32),
        ],
        compiler_params=pltpu.CompilerParams(vmem_limit_bytes=34 * MEBI),
        cost_estimate=pl.CostEstimate(flops=30_000_000, bytes_accessed=20_000_000, transcendentals=0),
    )(left, right, coef, forward, first_sums, stair)


def shards(adjoint_init, forward_state, p_speed, s_speed, density):
    init = adjoint_init[0]
    row = lax.axis_index("event").reshape(1)
    first, last, init, coef, own = run_prepare(row, init, jnp.stack([p_speed, s_speed, density]))
    count = lax.axis_size("lon")
    up = [(i, (i + 1) % count) for i in range(count)]
    left = lax.ppermute(last, "lon", up)
    right = lax.ppermute(first, "lon", [(j, i) for i, j in up])
    pairs = lax.axis_size("event") // 2
    first_sums, sent, kept, stair, forward = run_inner(row // pairs, init, coef, forward_state)
    swap = [(i, (i + pairs) % (2 * pairs)) for i in range(2 * pairs)]
    swapped = lax.ppermute(sent, "event", swap)
    ends = run_outer(left, right, coef, forward, first_sums, stair)
    partial = run_join(ends, kept, swapped)
    parts = lax.all_to_all(partial, "event", 0, 0, tiled=True)
    return run_finish(parts, own)


def solution(mesh):
    placed = (
        P("event", None, None, "lon", None),
        P("event", None, None, None, "lon", None),
        P(None, "lon", None),
        P(None, "lon", None),
        P(None, "lon", None),
    )
    return jax.shard_map(
        shards, mesh=mesh, in_specs=placed, out_specs=P(None, "event", "lon", None), check_vma=False
    )
```

```python
import functools

import jax
import jax.numpy as jnp
from jax import lax
from jax.experimental import pallas as pl
from jax.experimental.pallas import tpu as pltpu
from jax.sharding import PartitionSpec as P

F32, BF16 = jnp.float32, jnp.bfloat16
HALO = 8
PAD = 8
FRONT = 8
VX, VY, VZ, XX, YY, ZZ, XY, XZ, YZ = range(9)
LAME, SHEAR2, BUOY = range(3)


def before_lat(value):
    edge = lax.broadcasted_iota(jnp.int32, value.shape, 1) == 0
    return jnp.where(edge, 0.0, pltpu.roll(value, 1, 1))


def after_lat(value):
    edge = lax.broadcasted_iota(jnp.int32, value.shape, 1) == 127
    return jnp.where(edge, 0.0, pltpu.roll(value, 127, 1))


def rounded(value):
    return value.astype(BF16).astype(F32)


def push(at, put, buoy):
    x_buoy, shift, yz_buoy = buoy
    xy, xz = at(XY, 0, shift), at(XZ, 0, shift)
    xy_x, xz_x = at(XY, 0, 0), at(XZ, 0, 0)
    yz = at(YZ, 0, shift)
    force_x = (at(XX, 0, 1) - at(XX, 0, 0)) + (xy_x - before_lat(xy_x)) + (xz_x - at(XZ, -1, 0))
    yy = at(YY, 0, shift)
    force_y = (xy - at(XY, 0, shift - 1)) + (after_lat(yy) - yy) + (yz - at(YZ, -1, shift))
    force_z = (
        (xz - at(XZ, 0, shift - 1))
        + (yz - before_lat(yz))
        + (at(ZZ, 1, shift) - at(ZZ, 0, shift))
    )
    put(VX, 0, rounded(at(VX, 0, 0) + x_buoy * force_x))
    put(VY, shift, rounded(at(VY, 0, shift) + yz_buoy * force_y))
    put(VZ, shift, rounded(at(VZ, 0, shift) + yz_buoy * force_z))


def strain(at, put, lame, shear2):
    vx, vy, vz = at(VX, 0, 0), at(VY, 0, 0), at(VZ, 0, 0)
    e_xx = vx - at(VX, 0, -1)
    e_yy = vy - before_lat(vy)
    e_zz = vz - at(VZ, -1, 0)
    d_xy = (after_lat(vx) - vx) + (at(VY, 0, 1) - vy)
    d_xz = (at(VX, 1, 0) - vx) + (at(VZ, 0, 1) - vz)
    d_yz = (at(VY, 1, 0) - vy) + (after_lat(vz) - vz)
    trace = e_xx + e_yy + e_zz
    shear = 0.5 * shear2
    volume = lame * trace
    for field, change in (
        (XX, volume + shear2 * e_xx),
        (YY, volume + shear2 * e_yy),
        (ZZ, volume + shear2 * e_zz),
        (XY, shear * d_xy),
        (XZ, shear * d_xz),
        (YZ, shear * d_yz),
    ):
        put(field, 0, rounded(at(field, 0, 0) + change))
    return (vx, vy, vz), (e_xx, e_yy, e_zz, d_xy, d_xz, d_yz), trace


def terms(speed, rate, trace, f):
    return (
        trace * (f[3] + f[4] + f[5]),
        (rate[0] * f[3] + rate[1] * f[4] + rate[2] * f[5])
        + (rate[3] * f[6] + rate[4] * f[7] + rate[5] * f[8]),
        speed[0] * f[0] + speed[1] * f[1] + speed[2] * f[2],
    )


def inner(steps, levels, width, half, init, coef, forward_hbm, sums, sent, kept, stair, forward, state, arrived):
    step = pl.program_id(0)

    starts = (0, 1, 3)

    def fetch(group):
        begin = starts[group]
        part = pl.ds(begin, (starts + (steps,))[group + 1] - begin)
        return pltpu.make_async_copy(forward_hbm.at[0, part], forward.at[part], arrived.at[group])

    def keep(level, side, field, row, value):
        stair[side, field, level, pl.ds(row, 1)] = value

    @pl.when(step == 0)
    def _():
        fetch(0).start()
        empty = jnp.zeros((9, 1, width + 2 * PAD, 128), F32)
        state[:, pl.ds(0, 1)] = empty
        state[:, pl.ds(levels + 1, 1)] = empty

        def load(level, carry):
            for field in range(9):
                state[field, level + 1, pl.ds(0, PAD)] = jnp.zeros((PAD, 128), F32)
                state[field, level + 1, pl.ds(PAD + width, PAD)] = jnp.zeros((PAD, 128), F32)
                state[field, level + 1, pl.ds(PAD, width)] = init[field, level].astype(F32)
                if field != VX:
                    stair[0, field, level, pl.ds(0, 1)] = state[field, level + 1, pl.ds(PAD, 1)]
                if field not in (VY, VZ):
                    stair[1, field, level, pl.ds(15, 1)] = state[field, level + 1, pl.ds(PAD + width - 1, 1)]
            for which in range(3):
                sums[which, level] = jnp.zeros((width, 128), F32)
            return carry

        lax.fori_loop(0, levels, load, 0)
        for group in range(1, len(starts)):
            fetch(group).start()

    def view(level, start, rows):
        def at(field, lev, lon):
            return state[field, level + 1 + lev, pl.ds(PAD + start + lon, rows)]

        def put(field, lon, value):
            state[field, level + 1, pl.ds(PAD + start + lon, rows)] = value

        return at, put

    def velocity(level):
        for start in range(0, width, 16):
            buoy = coef[BUOY, level, pl.ds(start, 16)]
            push(*view(level, start, 16), (buoy, 0, buoy))
        for field in (VX, VY, VZ):
            first = step if field == VX else step + 1
            last = 30 - step if field == VX else 31 - step
            keep(level, 0, field, first, state[field, level + 1, pl.ds(PAD + first, 1)])
            keep(level, 1, field, last - 16, state[field, level + 1, pl.ds(PAD + last, 1)])

    def stress(level):
        for start in range(0, width, 16):
            mine = pl.ds(start, 16)
            parts = strain(*view(level, start, 16), coef[LAME, level, mine], coef[SHEAR2, level, mine])
            f = [forward[step, field, level, mine].astype(F32) for field in range(9)]
            column = lax.broadcasted_iota(jnp.int32, (8, 128), 0)
            for which, term in enumerate(terms(*parts, f)):
                if start == 0:
                    term = jnp.concatenate([jnp.where(column > step, term[:8], 0.0), term[8:]])
                elif start == width - 16:
                    term = jnp.concatenate([term[:8], jnp.where(column < 7 - step, term[8:], 0.0)])
                sums[which, level, mine] += term
        for field in range(3, 9):
            keep(level, 0, field, step + 1, state[field, level + 1, pl.ds(PAD + step + 1, 1)])
            keep(level, 1, field, 14 - step, state[field, level + 1, pl.ds(PAD + 30 - step, 1)])

    for group, begin in enumerate(starts):
        pl.when(step == begin)(fetch(group).wait)

    velocity(0)
    for level in range(levels):
        if level + 1 < levels:
            velocity(level + 1)
        stress(level)

    @pl.when(step == steps - 1)
    def _():
        mine = pl.multiple_of(8 + 8 * half[0], 8)
        other = pl.multiple_of(16 - 8 * half[0], 8)
        for level in range(levels):
            for which in range(3):
                kept[which, level] = sums[which, level, pl.ds(mine, 8)]
                sent[which, level] = sums[which, level, pl.ds(other, 8)].astype(BF16)


def outer(steps, levels, width, left, right, coef, forward, first_sums, stair, out, state, mat, sums, wide_f):
    step = pl.program_id(0)

    @pl.when(step == 0)
    def _():
        for side in range(2):
            empty = jnp.zeros((9, 1, 24, 128), F32)
            state[side, :, pl.ds(0, 1)] = empty
            state[side, :, pl.ds(levels + 1, 1)] = empty

        def load(level, carry):
            for field in range(9):
                state[0, field, level + 1, pl.ds(FRONT, 8)] = left[field, level].astype(F32)
                state[0, field, level + 1, pl.ds(FRONT + 8, 8)] = stair[0, field, level, pl.ds(0, 8)]
                state[1, field, level + 1, pl.ds(0, 8)] = stair[1, field, level, pl.ds(8, 8)]
                state[1, field, level + 1, pl.ds(FRONT, 8)] = right[field, level].astype(F32)
                wide_f[0, field, level, pl.ds(0, 8)] = jnp.zeros((8, 128), F32)
                wide_f[1, field, level, pl.ds(8, 8)] = jnp.zeros((8, 128), F32)
            for which in range(3):
                mat[0, which, level, pl.ds(0, 8)] = left[9 + which, level].astype(F32)
                mat[0, which, level, pl.ds(8, 16)] = coef[which, level, pl.ds(0, 16)]
                mat[1, which, level, pl.ds(0, 16)] = coef[which, level, pl.ds(width - 16, 16)]
                mat[1, which, level, pl.ds(16, 8)] = right[9 + which, level].astype(F32)
                for side in range(2):
                    sums[side, which, level] = jnp.zeros((24, 128), F32)
            return carry

        lax.fori_loop(0, levels, load, 0)

    def widen(level):
        for field in range(9):
            wide_f[0, field, level, pl.ds(8, 8)] = forward[step, field, level, pl.ds(0, 16)].astype(F32)[:8]
            wide_f[1, field, level, pl.ds(0, 8)] = forward[step, field, level, pl.ds(width - 16, 16)].astype(F32)[8:]

    for level in range(levels):
        widen(level)

    old_x, new_x, old_s = (0, -1), (-1, 0), (1, -1)
    x_coef, s_coef, f_row = (step, 15 - step), (step + 1, 15 - step), (step + 1, 7 - step)

    def velocity(level):
        for side in range(2):

            def at(field, lev, lon):
                return state[side, field, level + 1 + lev, pl.ds(FRONT + old_x[side] + lon, 8)]

            def put(field, lon, value):
                state[side, field, level + 1, pl.ds(FRONT + new_x[side] + lon, 8)] = value

            x_buoy = mat[side, BUOY, level, pl.ds(x_coef[side], 8)]
            yz_buoy = mat[side, BUOY, level, pl.ds(x_coef[side] + 1, 8)]
            push(at, put, (x_buoy, 1, yz_buoy))
        for field in (VX, VY, VZ):
            first, row = (step, 7) if field == VX else (step + 1, 8)
            state[0, field, level + 1, pl.ds(FRONT + row, 1)] = stair[0, field, level, pl.ds(first, 1)]
            last, row = (14 - step, -1) if field == VX else (15 - step, 0)
            state[1, field, level + 1, pl.ds(FRONT + row, 1)] = stair[1, field, level, pl.ds(last, 1)]

    def stress(level):
        for side in range(2):

            def at(field, lev, lon):
                row = FRONT + lon + (old_s[side] if field >= 3 else 0)
                return state[side, field, level + 1 + lev, pl.ds(row, 8)]

            def put(field, lon, value):
                state[side, field, level + 1, pl.ds(FRONT + lon, 8)] = value

            rows = pl.ds(s_coef[side], 8)
            parts = strain(at, put, mat[side, LAME, level, rows], mat[side, SHEAR2, level, rows])
            f = [wide_f[side, field, level, pl.ds(f_row[side], 8)] for field in range(9)]
            for which, term in enumerate(terms(*parts, f)):
                before = sums[side, which, level, pl.ds(8 + old_s[side], 8)]
                sums[side, which, level, pl.ds(8, 8)] = before + term
        for field in range(3, 9):
            state[0, field, level + 1, pl.ds(FRONT + 8, 1)] = stair[0, field, level, pl.ds(step + 1, 1)]
            state[1, field, level + 1, pl.ds(FRONT - 1, 1)] = stair[1, field, level, pl.ds(14 - step, 1)]

    velocity(0)
    for level in range(levels):
        if level + 1 < levels:
            velocity(level + 1)
        stress(level)

    @pl.when(step == steps - 1)
    def _():
        for level in range(levels):
            for which in range(3):
                for side, start in enumerate((0, width - 8)):
                    out[side, which, level] = sums[side, which, level, pl.ds(8, 8)] + first_sums[which, level, pl.ds(start, 8)]


def prepare(levels, width, row, init_hbm, material, first, last, init, coef, own, arrived):
    copy = pltpu.make_async_copy(init_hbm, init, arrived.at[0])
    copy.start()

    def materials(level, carry):
        p, s, rho = [material[which, level] for which in range(3)]
        parts = (rho * (p * p - 2.0 * s * s), 2.0 * rho * s * s, 1.0 / rho)
        for which, part in enumerate(parts):
            coef[which, level] = part
            first[9 + which, level] = part[:HALO].astype(BF16)
            last[9 + which, level] = part[width - HALO :].astype(BF16)
        return carry

    lax.fori_loop(0, levels, materials, 0, unroll=4)
    for which in range(3):
        own[which] = material[which, row[0]]
    copy.wait()

    def edges(level, carry):
        for field in range(9):
            first[field, level] = init[field, level, pl.ds(0, 16)].astype(F32)[:HALO].astype(BF16)
            last[field, level] = init[field, level, pl.ds(width - 16, 16)].astype(F32)[16 - HALO :].astype(BF16)
        return carry

    lax.fori_loop(0, levels, edges, 0, unroll=4)


def join(levels, ends, kept, swapped, out):
    for level in range(levels):
        for which, factor in enumerate((1.0, 2.0, 1.0)):
            quarter = kept[which, level] + swapped[which, level].astype(F32)
            both = [ends[side, which, level] for side in range(2)]
            out[level, which] = (factor * jnp.concatenate(both + [quarter])).astype(BF16)


def finish(events, parts, own, out):
    def summed(which, first, last):
        total = parts[first, which].astype(F32)
        for event in range(first + 1, last):
            total = total + parts[event, which].astype(F32)
        return total

    half = events // 2
    total = []
    for which in range(3):
        low, high = summed(which, 0, half), summed(which, half, events)
        ends = low[:16] + high[:16]
        total.append(jnp.concatenate([ends[:8], low[16:], high[16:], ends[8:]]))
    p_speed, s_speed, density = own[0], own[1], own[2]
    lame = density * (p_speed * p_speed - 2.0 * s_speed * s_speed)
    shear = density * s_speed * s_speed
    out[0, 0] = 2.0 * density * p_speed * p_speed * total[0]
    out[1, 0] = 2.0 * density * s_speed * s_speed * (total[1] - 2.0 * total[0])
    out[2, 0] = density * total[2] + lame * total[0] + shear * total[1]


IN_VMEM = pl.BlockSpec(memory_space=pltpu.VMEM)
IN_HBM = pl.BlockSpec(memory_space=pltpu.HBM)
MEBI = 1024 * 1024


def run_prepare(row, init, material):
    _, levels, width, lat = init.shape
    edge = jax.ShapeDtypeStruct((12, levels, HALO, lat), BF16)
    return pl.pallas_call(
        functools.partial(prepare, levels, width),
        in_specs=[pl.BlockSpec(memory_space=pltpu.SMEM)] + [IN_HBM, IN_VMEM],
        out_specs=[IN_VMEM] * 5,
        out_shape=[
            edge,
            edge,
            jax.ShapeDtypeStruct(init.shape, BF16),
            jax.ShapeDtypeStruct((3, levels, width, lat), F32),
            jax.ShapeDtypeStruct((3, width, lat), F32),
        ],
        scratch_shapes=[pltpu.SemaphoreType.DMA((1,))],
        compiler_params=pltpu.CompilerParams(vmem_limit_bytes=50 * MEBI),
    )(row, init, material)


def run_join(ends, kept, swapped):
    _, levels, _, lat = kept.shape
    return pl.pallas_call(
        functools.partial(join, levels),
        in_specs=[IN_VMEM] * 3,
        out_specs=IN_VMEM,
        out_shape=jax.ShapeDtypeStruct((levels, 3, 24, lat), BF16),
        compiler_params=pltpu.CompilerParams(vmem_limit_bytes=8 * MEBI),
    )(ends, kept, swapped)


def run_finish(parts, own):
    events, _, _, lat = parts.shape
    width = own.shape[1]
    return pl.pallas_call(
        functools.partial(finish, events),
        in_specs=[IN_VMEM] * 2,
        out_specs=IN_VMEM,
        out_shape=jax.ShapeDtypeStruct((3, 1, width, lat), F32),
        compiler_params=pltpu.CompilerParams(vmem_limit_bytes=8 * MEBI),
    )(parts, own)


def run_inner(half, init, coef, forward):
    _, steps, _, levels, width, lat = forward.shape
    outs = [
        jax.ShapeDtypeStruct((3, levels, width, lat), F32),
        jax.ShapeDtypeStruct((3, levels, 8, lat), BF16),
        jax.ShapeDtypeStruct((3, levels, 8, lat), F32),
        jax.ShapeDtypeStruct((2, 9, levels, 16, lat), F32),
        jax.ShapeDtypeStruct(forward.shape[1:], BF16),
    ]
    return pl.pallas_call(
        functools.partial(inner, steps, levels, width),
        grid=(steps,),
        in_specs=[pl.BlockSpec(memory_space=pltpu.SMEM), IN_VMEM, IN_VMEM, IN_HBM],
        out_specs=[IN_VMEM] * 5,
        out_shape=outs,
        scratch_shapes=[
            pltpu.VMEM((9, levels + 2, width + 2 * PAD, lat), F32),
            pltpu.SemaphoreType.DMA((3,)),
        ],
        compiler_params=pltpu.CompilerParams(vmem_limit_bytes=34 * MEBI),
        cost_estimate=pl.CostEstimate(flops=60_000_000, bytes_accessed=30_000_000, transcendentals=0),
    )(half, init, coef, forward)


def run_outer(left, right, coef, forward, first_sums, stair):
    steps, _, levels, width, lat = forward.shape
    return pl.pallas_call(
        functools.partial(outer, steps, levels, width),
        grid=(steps,),
        in_specs=[IN_VMEM] * 6,
        out_specs=IN_VMEM,
        out_shape=jax.ShapeDtypeStruct((2, 3, levels, 8, lat), F32),
        scratch_shapes=[
            pltpu.VMEM((2, 9, levels + 2, 24, lat), F32),
            pltpu.VMEM((2, 3, levels, 24, lat), F32),
            pltpu.VMEM((2, 3, levels, 24, lat), F32),
            pltpu.VMEM((2, 9, levels, 16, lat), F32),
        ],
        compiler_params=pltpu.CompilerParams(vmem_limit_bytes=34 * MEBI),
        cost_estimate=pl.CostEstimate(flops=30_000_000, bytes_accessed=20_000_000, transcendentals=0),
    )(left, right, coef, forward, first_sums, stair)


def shards(adjoint_init, forward_state, p_speed, s_speed, density):
    init = adjoint_init[0]
    row = lax.axis_index("event").reshape(1)
    first, last, init, coef, own = run_prepare(row, init, jnp.stack([p_speed, s_speed, density]))
    count = lax.axis_size("lon")
    up = [(i, (i + 1) % count) for i in range(count)]
    left = lax.ppermute(last, "lon", up)
    right = lax.ppermute(first, "lon", [(j, i) for i, j in up])
    pairs = lax.axis_size("event") // 2
    first_sums, sent, kept, stair, forward = run_inner(row // pairs, init, coef, forward_state)
    swap = [(i, (i + pairs) % (2 * pairs)) for i in range(2 * pairs)]
    swapped = lax.ppermute(sent, "event", swap)
    ends = run_outer(left, right, coef, forward, first_sums, stair)
    partial = run_join(ends, kept, swapped)
    parts = lax.all_to_all(partial, "event", 0, 0, tiled=True)
    return run_finish(parts, own)


def solution(mesh):
    placed = (
        P("event", None, None, "lon", None),
        P("event", None, None, None, "lon", None),
        P(None, "lon", None),
        P(None, "lon", None),
        P(None, "lon", None),
    )
    return jax.shard_map(
        shards, mesh=mesh, in_specs=placed, out_specs=P(None, "event", "lon", None), check_vma=False
    )
```

```python
import functools

import jax
import jax.numpy as jnp
from jax import lax
from jax.experimental import pallas as pl
from jax.experimental.pallas import tpu as pltpu
from jax.sharding import PartitionSpec as P

F32, BF16 = jnp.float32, jnp.bfloat16
HALO = 8
PAD = 8
FRONT = 8
VX, VY, VZ, XX, YY, ZZ, XY, XZ, YZ = range(9)
LAME, SHEAR2, BUOY = range(3)


def before_lat(value):
    edge = lax.broadcasted_iota(jnp.int32, value.shape, 1) == 0
    return jnp.where(edge, 0.0, pltpu.roll(value, 1, 1))


def after_lat(value):
    edge = lax.broadcasted_iota(jnp.int32, value.shape, 1) == 127
    return jnp.where(edge, 0.0, pltpu.roll(value, 127, 1))


def rounded(value):
    return value.astype(BF16).astype(F32)


def push(at, put, buoy):
    x_buoy, shift, yz_buoy = buoy
    xy, xz = at(XY, 0, shift), at(XZ, 0, shift)
    xy_x, xz_x = at(XY, 0, 0), at(XZ, 0, 0)
    yz = at(YZ, 0, shift)
    force_x = (at(XX, 0, 1) - at(XX, 0, 0)) + (xy_x - before_lat(xy_x)) + (xz_x - at(XZ, -1, 0))
    yy = at(YY, 0, shift)
    force_y = (xy - at(XY, 0, shift - 1)) + (after_lat(yy) - yy) + (yz - at(YZ, -1, shift))
    force_z = (
        (xz - at(XZ, 0, shift - 1))
        + (yz - before_lat(yz))
        + (at(ZZ, 1, shift) - at(ZZ, 0, shift))
    )
    put(VX, 0, rounded(at(VX, 0, 0) + x_buoy * force_x))
    put(VY, shift, rounded(at(VY, 0, shift) + yz_buoy * force_y))
    put(VZ, shift, rounded(at(VZ, 0, shift) + yz_buoy * force_z))


def strain(at, put, lame, shear2):
    vx, vy, vz = at(VX, 0, 0), at(VY, 0, 0), at(VZ, 0, 0)
    e_xx = vx - at(VX, 0, -1)
    e_yy = vy - before_lat(vy)
    e_zz = vz - at(VZ, -1, 0)
    d_xy = (after_lat(vx) - vx) + (at(VY, 0, 1) - vy)
    d_xz = (at(VX, 1, 0) - vx) + (at(VZ, 0, 1) - vz)
    d_yz = (at(VY, 1, 0) - vy) + (after_lat(vz) - vz)
    trace = e_xx + e_yy + e_zz
    shear = 0.5 * shear2
    volume = lame * trace
    for field, change in (
        (XX, volume + shear2 * e_xx),
        (YY, volume + shear2 * e_yy),
        (ZZ, volume + shear2 * e_zz),
        (XY, shear * d_xy),
        (XZ, shear * d_xz),
        (YZ, shear * d_yz),
    ):
        put(field, 0, rounded(at(field, 0, 0) + change))
    return (vx, vy, vz), (e_xx, e_yy, e_zz, d_xy, d_xz, d_yz), trace


def terms(speed, rate, trace, f):
    return (
        trace * (f[3] + f[4] + f[5]),
        (rate[0] * f[3] + rate[1] * f[4] + rate[2] * f[5])
        + (rate[3] * f[6] + rate[4] * f[7] + rate[5] * f[8]),
        speed[0] * f[0] + speed[1] * f[1] + speed[2] * f[2],
    )


def inner(steps, levels, width, half, init, coef, forward_hbm, sums, sent, kept, stair, forward, state, arrived):
    step = pl.program_id(0)

    starts = (0, 1, 3)

    def fetch(group):
        begin = starts[group]
        part = pl.ds(begin, (starts + (steps,))[group + 1] - begin)
        return pltpu.make_async_copy(forward_hbm.at[0, part], forward.at[part], arrived.at[group])

    def keep(level, side, field, row, value):
        stair[side, field, level, pl.ds(row, 1)] = value

    @pl.when(step == 0)
    def _():
        fetch(0).start()
        empty = jnp.zeros((9, 1, width + 2 * PAD, 128), F32)
        state[:, pl.ds(0, 1)] = empty
        state[:, pl.ds(levels + 1, 1)] = empty

        def load(level, carry):
            for field in range(9):
                state[field, level + 1, pl.ds(0, PAD)] = jnp.zeros((PAD, 128), F32)
                state[field, level + 1, pl.ds(PAD + width, PAD)] = jnp.zeros((PAD, 128), F32)
                state[field, level + 1, pl.ds(PAD, width)] = init[field, level].astype(F32)
                if field != VX:
                    stair[0, field, level, pl.ds(0, 1)] = state[field, level + 1, pl.ds(PAD, 1)]
                if field not in (VY, VZ):
                    stair[1, field, level, pl.ds(15, 1)] = state[field, level + 1, pl.ds(PAD + width - 1, 1)]
            for which in range(3):
                sums[which, level] = jnp.zeros((width, 128), F32)
            return carry

        lax.fori_loop(0, levels, load, 0)
        for group in range(1, len(starts)):
            fetch(group).start()

    def view(level, start, rows):
        def at(field, lev, lon):
            return state[field, level + 1 + lev, pl.ds(PAD + start + lon, rows)]

        def put(field, lon, value):
            state[field, level + 1, pl.ds(PAD + start + lon, rows)] = value

        return at, put

    def velocity(level):
        for start in range(0, width, 16):
            buoy = coef[BUOY, level, pl.ds(start, 16)]
            push(*view(level, start, 16), (buoy, 0, buoy))
        for field in (VX, VY, VZ):
            first = step if field == VX else step + 1
            last = 30 - step if field == VX else 31 - step
            keep(level, 0, field, first, state[field, level + 1, pl.ds(PAD + first, 1)])
            keep(level, 1, field, last - 16, state[field, level + 1, pl.ds(PAD + last, 1)])

    def stress(level):
        for start in range(0, width, 16):
            mine = pl.ds(start, 16)
            parts = strain(*view(level, start, 16), coef[LAME, level, mine], coef[SHEAR2, level, mine])
            f = [forward[step, field, level, mine].astype(F32) for field in range(9)]
            column = lax.broadcasted_iota(jnp.int32, (8, 128), 0)
            for which, term in enumerate(terms(*parts, f)):
                if start == 0:
                    term = jnp.concatenate([jnp.where(column > step, term[:8], 0.0), term[8:]])
                elif start == width - 16:
                    term = jnp.concatenate([term[:8], jnp.where(column < 7 - step, term[8:], 0.0)])
                sums[which, level, mine] += term
        for field in range(3, 9):
            keep(level, 0, field, step + 1, state[field, level + 1, pl.ds(PAD + step + 1, 1)])
            keep(level, 1, field, 14 - step, state[field, level + 1, pl.ds(PAD + 30 - step, 1)])

    for level in range(levels):
        velocity(level)
    for group, begin in enumerate(starts):
        pl.when(step == begin)(fetch(group).wait)
    for level in range(levels):
        stress(level)

    @pl.when(step == steps - 1)
    def _():
        mine = pl.multiple_of(8 + 8 * half[0], 8)
        other = pl.multiple_of(16 - 8 * half[0], 8)
        for level in range(levels):
            for which in range(3):
                kept[which, level] = sums[which, level, pl.ds(mine, 8)]
                sent[which, level] = sums[which, level, pl.ds(other, 8)].astype(BF16)


def outer(steps, levels, width, left, right, coef, forward, first_sums, stair, out, state, mat, sums, wide_f):
    step = pl.program_id(0)

    @pl.when(step == 0)
    def _():
        for side in range(2):
            empty = jnp.zeros((9, 1, 24, 128), F32)
            state[side, :, pl.ds(0, 1)] = empty
            state[side, :, pl.ds(levels + 1, 1)] = empty

        def load(level, carry):
            for field in range(9):
                state[0, field, level + 1, pl.ds(FRONT, 8)] = left[field, level].astype(F32)
                state[0, field, level + 1, pl.ds(FRONT + 8, 8)] = stair[0, field, level, pl.ds(0, 8)]
                state[1, field, level + 1, pl.ds(0, 8)] = stair[1, field, level, pl.ds(8, 8)]
                state[1, field, level + 1, pl.ds(FRONT, 8)] = right[field, level].astype(F32)
                wide_f[0, field, level, pl.ds(0, 8)] = jnp.zeros((8, 128), F32)
                wide_f[1, field, level, pl.ds(8, 8)] = jnp.zeros((8, 128), F32)
            for which in range(3):
                mat[0, which, level, pl.ds(0, 8)] = left[9 + which, level].astype(F32)
                mat[0, which, level, pl.ds(8, 16)] = coef[which, level, pl.ds(0, 16)]
                mat[1, which, level, pl.ds(0, 16)] = coef[which, level, pl.ds(width - 16, 16)]
                mat[1, which, level, pl.ds(16, 8)] = right[9 + which, level].astype(F32)
                for side in range(2):
                    sums[side, which, level] = jnp.zeros((24, 128), F32)
            return carry

        lax.fori_loop(0, levels, load, 0)

    def widen(level):
        for field in range(9):
            wide_f[0, field, level, pl.ds(8, 8)] = forward[step, field, level, pl.ds(0, 16)].astype(F32)[:8]
            wide_f[1, field, level, pl.ds(0, 8)] = forward[step, field, level, pl.ds(width - 16, 16)].astype(F32)[8:]

    for level in range(levels):
        widen(level)

    old_x, new_x, old_s = (0, -1), (-1, 0), (1, -1)
    x_coef, s_coef, f_row = (step, 15 - step), (step + 1, 15 - step), (step + 1, 7 - step)

    def velocity(level):
        for side in range(2):

            def at(field, lev, lon):
                return state[side, field, level + 1 + lev, pl.ds(FRONT + old_x[side] + lon, 8)]

            def put(field, lon, value):
                state[side, field, level + 1, pl.ds(FRONT + new_x[side] + lon, 8)] = value

            x_buoy = mat[side, BUOY, level, pl.ds(x_coef[side], 8)]
            yz_buoy = mat[side, BUOY, level, pl.ds(x_coef[side] + 1, 8)]
            push(at, put, (x_buoy, 1, yz_buoy))
        for field in (VX, VY, VZ):
            first, row = (step, 7) if field == VX else (step + 1, 8)
            state[0, field, level + 1, pl.ds(FRONT + row, 1)] = stair[0, field, level, pl.ds(first, 1)]
            last, row = (14 - step, -1) if field == VX else (15 - step, 0)
            state[1, field, level + 1, pl.ds(FRONT + row, 1)] = stair[1, field, level, pl.ds(last, 1)]

    def stress(level):
        for side in range(2):

            def at(field, lev, lon):
                row = FRONT + lon + (old_s[side] if field >= 3 else 0)
                return state[side, field, level + 1 + lev, pl.ds(row, 8)]

            def put(field, lon, value):
                state[side, field, level + 1, pl.ds(FRONT + lon, 8)] = value

            rows = pl.ds(s_coef[side], 8)
            parts = strain(at, put, mat[side, LAME, level, rows], mat[side, SHEAR2, level, rows])
            f = [wide_f[side, field, level, pl.ds(f_row[side], 8)] for field in range(9)]
            for which, term in enumerate(terms(*parts, f)):
                before = sums[side, which, level, pl.ds(8 + old_s[side], 8)]
                sums[side, which, level, pl.ds(8, 8)] = before + term
        for field in range(3, 9):
            state[0, field, level + 1, pl.ds(FRONT + 8, 1)] = stair[0, field, level, pl.ds(step + 1, 1)]
            state[1, field, level + 1, pl.ds(FRONT - 1, 1)] = stair[1, field, level, pl.ds(14 - step, 1)]

    velocity(0)
    for level in range(levels):
        if level + 1 < levels:
            velocity(level + 1)
        stress(level)

    @pl.when(step == steps - 1)
    def _():
        for level in range(levels):
            for which in range(3):
                for side, start in enumerate((0, width - 8)):
                    out[side, which, level] = sums[side, which, level, pl.ds(8, 8)] + first_sums[which, level, pl.ds(start, 8)]


def prepare(levels, width, row, init_hbm, material, first, last, init, coef, own, arrived):
    copy = pltpu.make_async_copy(init_hbm, init, arrived.at[0])
    copy.start()

    def materials(level, carry):
        p, s, rho = [material[which, level] for which in range(3)]
        parts = (rho * (p * p - 2.0 * s * s), 2.0 * rho * s * s, 1.0 / rho)
        for which, part in enumerate(parts):
            coef[which, level] = part
            first[9 + which, level] = part[:HALO].astype(BF16)
            last[9 + which, level] = part[width - HALO :].astype(BF16)
        return carry

    lax.fori_loop(0, levels, materials, 0, unroll=4)
    for which in range(3):
        own[which] = material[which, row[0]]
    copy.wait()

    def edges(level, carry):
        for field in range(9):
            first[field, level] = init[field, level, pl.ds(0, 16)].astype(F32)[:HALO].astype(BF16)
            last[field, level] = init[field, level, pl.ds(width - 16, 16)].astype(F32)[16 - HALO :].astype(BF16)
        return carry

    lax.fori_loop(0, levels, edges, 0, unroll=4)


def join(levels, ends, kept, swapped, out):
    for level in range(levels):
        for which, factor in enumerate((1.0, 2.0, 1.0)):
            quarter = kept[which, level] + swapped[which, level].astype(F32)
            both = [ends[side, which, level] for side in range(2)]
            out[level, which] = (factor * jnp.concatenate(both + [quarter])).astype(BF16)


def finish(events, parts, own, out):
    def summed(which, first, last):
        total = parts[first, which].astype(F32)
        for event in range(first + 1, last):
            total = total + parts[event, which].astype(F32)
        return total

    half = events // 2
    total = []
    for which in range(3):
        low, high = summed(which, 0, half), summed(which, half, events)
        ends = low[:16] + high[:16]
        total.append(jnp.concatenate([ends[:8], low[16:], high[16:], ends[8:]]))
    p_speed, s_speed, density = own[0], own[1], own[2]
    lame = density * (p_speed * p_speed - 2.0 * s_speed * s_speed)
    shear = density * s_speed * s_speed
    out[0, 0] = 2.0 * density * p_speed * p_speed * total[0]
    out[1, 0] = 2.0 * density * s_speed * s_speed * (total[1] - 2.0 * total[0])
    out[2, 0] = density * total[2] + lame * total[0] + shear * total[1]


IN_VMEM = pl.BlockSpec(memory_space=pltpu.VMEM)
IN_HBM = pl.BlockSpec(memory_space=pltpu.HBM)
MEBI = 1024 * 1024


def run_prepare(row, init, material):
    _, levels, width, lat = init.shape
    edge = jax.ShapeDtypeStruct((12, levels, HALO, lat), BF16)
    return pl.pallas_call(
        functools.partial(prepare, levels, width),
        in_specs=[pl.BlockSpec(memory_space=pltpu.SMEM)] + [IN_HBM, IN_VMEM],
        out_specs=[IN_VMEM] * 5,
        out_shape=[
            edge,
            edge,
            jax.ShapeDtypeStruct(init.shape, BF16),
            jax.ShapeDtypeStruct((3, levels, width, lat), F32),
            jax.ShapeDtypeStruct((3, width, lat), F32),
        ],
        scratch_shapes=[pltpu.SemaphoreType.DMA((1,))],
        compiler_params=pltpu.CompilerParams(vmem_limit_bytes=50 * MEBI),
    )(row, init, material)


def run_join(ends, kept, swapped):
    _, levels, _, lat = kept.shape
    return pl.pallas_call(
        functools.partial(join, levels),
        in_specs=[IN_VMEM] * 3,
        out_specs=IN_VMEM,
        out_shape=jax.ShapeDtypeStruct((levels, 3, 24, lat), BF16),
        compiler_params=pltpu.CompilerParams(vmem_limit_bytes=8 * MEBI),
    )(ends, kept, swapped)


def run_finish(parts, own):
    events, _, _, lat = parts.shape
    width = own.shape[1]
    return pl.pallas_call(
        functools.partial(finish, events),
        in_specs=[IN_VMEM] * 2,
        out_specs=IN_VMEM,
        out_shape=jax.ShapeDtypeStruct((3, 1, width, lat), F32),
        compiler_params=pltpu.CompilerParams(vmem_limit_bytes=8 * MEBI),
    )(parts, own)


def run_inner(half, init, coef, forward):
    _, steps, _, levels, width, lat = forward.shape
    outs = [
        jax.ShapeDtypeStruct((3, levels, width, lat), F32),
        jax.ShapeDtypeStruct((3, levels, 8, lat), BF16),
        jax.ShapeDtypeStruct((3, levels, 8, lat), F32),
        jax.ShapeDtypeStruct((2, 9, levels, 16, lat), F32),
        jax.ShapeDtypeStruct(forward.shape[1:], BF16),
    ]
    return pl.pallas_call(
        functools.partial(inner, steps, levels, width),
        grid=(steps,),
        in_specs=[pl.BlockSpec(memory_space=pltpu.SMEM), IN_VMEM, IN_VMEM, IN_HBM],
        out_specs=[IN_VMEM] * 5,
        out_shape=outs,
        scratch_shapes=[
            pltpu.VMEM((9, levels + 2, width + 2 * PAD, lat), F32),
            pltpu.SemaphoreType.DMA((3,)),
        ],
        compiler_params=pltpu.CompilerParams(vmem_limit_bytes=34 * MEBI),
        cost_estimate=pl.CostEstimate(flops=60_000_000, bytes_accessed=30_000_000, transcendentals=0),
    )(half, init, coef, forward)


def run_outer(left, right, coef, forward, first_sums, stair):
    steps, _, levels, width, lat = forward.shape
    return pl.pallas_call(
        functools.partial(outer, steps, levels, width),
        grid=(steps,),
        in_specs=[IN_VMEM] * 6,
        out_specs=IN_VMEM,
        out_shape=jax.ShapeDtypeStruct((2, 3, levels, 8, lat), F32),
        scratch_shapes=[
            pltpu.VMEM((2, 9, levels + 2, 24, lat), F32),
            pltpu.VMEM((2, 3, levels, 24, lat), F32),
            pltpu.VMEM((2, 3, levels, 24, lat), F32),
            pltpu.VMEM((2, 9, levels, 16, lat), F32),
        ],
        compiler_params=pltpu.CompilerParams(vmem_limit_bytes=34 * MEBI),
        cost_estimate=pl.CostEstimate(flops=30_000_000, bytes_accessed=20_000_000, transcendentals=0),
    )(left, right, coef, forward, first_sums, stair)


def shards(adjoint_init, forward_state, p_speed, s_speed, density):
    init = adjoint_init[0]
    row = lax.axis_index("event").reshape(1)
    first, last, init, coef, own = run_prepare(row, init, jnp.stack([p_speed, s_speed, density]))
    count = lax.axis_size("lon")
    up = [(i, (i + 1) % count) for i in range(count)]
    left = lax.ppermute(last, "lon", up)
    right = lax.ppermute(first, "lon", [(j, i) for i, j in up])
    pairs = lax.axis_size("event") // 2
    first_sums, sent, kept, stair, forward = run_inner(row // pairs, init, coef, forward_state)
    swap = [(i, (i + pairs) % (2 * pairs)) for i in range(2 * pairs)]
    swapped = lax.ppermute(sent, "event", swap)
    ends = run_outer(left, right, coef, forward, first_sums, stair)
    partial = run_join(ends, kept, swapped)
    parts = lax.all_to_all(partial, "event", 0, 0, tiled=True)
    return run_finish(parts, own)


def solution(mesh):
    placed = (
        P("event", None, None, "lon", None),
        P("event", None, None, None, "lon", None),
        P(None, "lon", None),
        P(None, "lon", None),
        P(None, "lon", None),
    )
    return jax.shard_map(
        shards, mesh=mesh, in_specs=placed, out_specs=P(None, "event", "lon", None), check_vma=False
    )
```
